32 devices in a mesh: tm: 4 (over x, core), cols: 8 (over z, y).
Axes of the slice: x: 2, y: 2, z: 4, core: 2. Of those that a mesh axis runs over, the one named last changes fastest.
Arguments:
- inv_diag: bfloat16 [4, 2048, 2048], P('tm', 'cols'), as said below
- sub_diag: bfloat16 [4, 2048, 2048], P('tm', 'cols'), may hold values from -0.09375 to 0.09375
- rhs: bfloat16 [4, 2048, 4096], P('tm', None, 'cols'), may hold values from -6 to 6
- carry_in: bfloat16 [2048, 4096], P(None, 'cols'), may hold values from -6 to 6
Outputs:
- solved: float32 [4, 2048, 4096], P('tm', None, 'cols')
The draws below stay inside these ranges and needn't reach their ends.
Inputs may be any that keep to these rules, and one draw needn't show every extreme that they name: Each block of inv_diag is lower triangular with diagonal entries between 0.5 and 1.5.
All inputs are finite; a program needn't handle non-finite values.
Results may differ from the reference program's by a relative error of at most 0.007.
Values may be sent and summed in bfloat16 or wider, within the bound.
A program may use at most 128 MiB of HBM per device.

```python
import jax
import jax.numpy as jnp
from jax import lax

BLOCK = 2048
BLOCKS = 4
SAMPLES = 4096


def draw_inv_diag(key, part):
    key_off = jax.random.fold_in(key, 11)
    key_diag = jax.random.fold_in(key, 12)
    spread_part = jax.random.normal(key_off, (BLOCKS, BLOCK, BLOCK), jnp.float32)
    diag_part = jax.random.uniform(key_diag, (BLOCKS, BLOCK), jnp.float32, 0.5, 1.5)
    spread_part = spread_part * (0.7 / jnp.sqrt(jnp.float32(BLOCK)))
    row_ids = lax.broadcasted_iota(jnp.int32, (BLOCK, BLOCK), 0)
    col_ids = lax.broadcasted_iota(jnp.int32, (BLOCK, BLOCK), 1)
    below_diag = jnp.where(row_ids > col_ids, spread_part, 0.0)
    on_diag = jnp.where(row_ids == col_ids, diag_part[:, :, None], 0.0)
    return (below_diag + on_diag).astype(jnp.bfloat16)


def levels(rng, shape, shards, low, high):
    def one(dim, shards_of):
        steps = jax.random.uniform(jax.random.fold_in(jax.random.fold_in(rng, 6), dim), (shards_of,), jnp.float32, low / len(shards), high / len(shards))
        return jnp.repeat(jnp.exp(steps), shape[dim] // shards_of).reshape((-1,) + (1,) * (len(shape) - dim - 1))

    gain = one(*shards[0])
    for cut in shards[1:]:
        gain = gain * one(*cut)
    return gain


def centred(rng, dims, scale, most, cuts=(), held_as=jnp.bfloat16):
    level = levels(rng, dims, cuts, -0.22, 0.18) if cuts else 1.0
    values = jax.random.normal(rng, dims, jnp.float32) * scale * level
    return jnp.minimum(jnp.maximum(values, -most), most).astype(held_as)


def setup_inputs(seed: int = 0) -> dict:
    keys = jax.random.split(jax.random.key(seed), 5)
    return {
        "inv_diag": draw_inv_diag(jax.random.fold_in(keys[4], 71), 0),
        "sub_diag": centred(keys[1], (BLOCKS, BLOCK, BLOCK), (2 * BLOCK) ** -0.5, 0.09375, ((0, 4), (1, 8))),
        "rhs": centred(keys[2], (BLOCKS, BLOCK, SAMPLES), 1.0, 6.0, ((0, 4), (2, 8))),
        "carry_in": centred(keys[3], (BLOCK, SAMPLES), 1.0, 6.0, ((1, 8),)),
    }


def advance(previous, inputs):
    inv_blk, sub_blk, source = inputs
    coupled = jnp.dot(sub_blk, previous, preferred_element_type=jnp.float32)
    update = (source.astype(jnp.float32) - coupled).astype(jnp.bfloat16)
    result = jnp.dot(inv_blk, update, preferred_element_type=jnp.float32)
    return result.astype(jnp.bfloat16), result


def reference(inv_diag, sub_diag, rhs, carry_in):
    final_block, solved = lax.scan(advance, carry_in, (inv_diag, sub_diag, rhs))
    return solved
```

```python
import functools

import jax
import jax.numpy as jnp
from jax import lax
from jax.experimental import pallas as pl
from jax.experimental.pallas import tpu as pltpu
from jax.sharding import PartitionSpec as P

MESH = pl.DeviceIdType.MESH
WIDE = 512
UP, DOWN, ACROSS, PAIR = 0, 1, 2, 3


def kernel(stages, lines, inv_ref, sub_ref, rhs_ref, carry_ref, out_ref,
           factors, rhs, prior, update, middle, last, solved,
           own_sem, give_send, give_recv, rhs_sem, carry_sem,
           send_sem, recv_sem, pair_sem, store_sem, out_send, out_recv, prior_send, prior_recv):
    section = lax.axis_index("tm")
    col = lax.axis_index("cols")
    stage, core = section // 2, lax.rem(section, 2)
    z, y = col // 2, lax.rem(col, 2)
    rows, order = inv_ref.shape[1], inv_ref.shape[2]
    half = rhs_ref.shape[2] // 2
    part, plane, pieces = rows // 2, 2 * rows, order // WIDE
    sibling = {"tm": 2 * stage + 1 - core}

    def if_(cond, fn):
        pl.when(cond)(fn)

    def each(count, fn):
        def body(j, carry):
            fn(j)
            return carry
        lax.fori_loop(0, count, body, 0)

    mine = pl.ds(pl.multiple_of(col * rows, rows), rows)

    def own(arr):
        return pltpu.make_async_copy((sub_ref, inv_ref)[arr].at[0], factors.at[2 * core + arr, mine, :], own_sem.at[arr])

    def given(arr, owner):
        return pltpu.make_async_remote_copy(
            src_ref=(sub_ref, inv_ref)[arr].at[0], dst_ref=factors.at[2 * owner + arr, mine, :],
            send_sem=give_send.at[arr], recv_sem=give_recv.at[arr], device_id=sibling, device_id_type=MESH)

    def half_of(c):
        return pl.ds(pl.multiple_of(c * half, half), half)

    own_rhs = pltpu.make_async_copy(rhs_ref.at[0, :, half_of(core)], rhs.at[core], rhs_sem)

    def given_rhs(owner):
        return pltpu.make_async_remote_copy(
            src_ref=rhs_ref.at[0, :, half_of(1 - core)], dst_ref=rhs.at[owner],
            send_sem=give_send.at[2], recv_sem=give_recv.at[2], device_id=sibling, device_id_type=MESH)

    own_carry = pltpu.make_async_copy(carry_ref.at[:, half_of(core)], prior, carry_sem)

    own(0).start()
    own(1).start()

    barrier = pltpu.get_barrier_semaphore()

    def greet(cond, device):
        @pl.when(cond)
        def _():
            pl.semaphore_signal(barrier, inc=1, device_id=device, device_id_type=MESH)

    greet(z > 0, {"cols": col - 2})
    greet(z < lines - 1, {"cols": col + 2})
    pl.semaphore_signal(barrier, inc=1, device_id={"cols": 2 * z + 1 - y}, device_id_type=MESH)
    pl.semaphore_signal(barrier, inc=1, device_id=sibling, device_id_type=MESH)
    greet(stage > 0, {"tm": section - 2})
    greet(stage < stages - 1, {"tm": section + 2})
    ends = [z > 0, z < lines - 1, stage > 0, stage < stages - 1]
    pl.semaphore_wait(barrier, 2 + sum(jnp.where(end, 1, 0) for end in ends))

    given(0, core).start()
    given(1, core).start()
    own_rhs.start()
    given_rhs(core).start()
    if_(stage == 0, own_carry.start)

    def blocks(s, z0):
        return pieces if s % 2 == 0 else (z0 * plane) // WIDE + 1

    def nth(s, k):
        return lax.rem(k + pieces - 1, pieces) if s % 2 == 0 else k

    def turned(s, y0):
        return False if s % 2 == 1 else (True if s == 0 else y0 == 1)

    def piece(s, c, j, h):
        return factors.at[s, pl.ds(pl.multiple_of(c * rows + h * part, part), part),
                          pl.ds(pl.multiple_of(j * WIDE, WIDE), WIDE)]

    def hop(way, s, c, j):
        ref = piece(s, c, j, core)
        to = ({"cols": col + 2}, {"cols": col - 2}, {"cols": 2 * z + 1 - y}, sibling)[way]
        return pltpu.make_async_remote_copy(
            src_ref=ref, dst_ref=ref, send_sem=send_sem.at[way, s, c, j],
            recv_sem=pair_sem.at[s, c, j] if way == PAIR else recv_sem.at[s, c, j], device_id=to, device_id_type=MESH)

    def paired(s, c, j):
        ref = piece(s, c, j, 1 - core)
        return pltpu.make_async_remote_copy(
            src_ref=ref, dst_ref=ref, send_sem=send_sem.at[PAIR, s, c, j],
            recv_sem=pair_sem.at[s, c, j], device_id=sibling, device_id_type=MESH)

    def along(act, s, c, j, up, down):
        if up:
            if_(z < lines - 1, lambda: act(hop(UP, s, c, j)))
        if down:
            if_(z > 0, lambda: act(hop(DOWN, s, c, j)))

    def sides(d, fn):
        if_(z - d >= 0, lambda: fn(z - d, True))
        if_(z + d < lines, lambda: fn(z + d, False))

    def own_sends(s, act):
        def one(k):
            j = nth(s, k)
            act(hop(ACROSS, s, col, j))
            along(act, s, col, j, True, True)
        each(blocks(s, z), one)

    def turn(s, act, arrive):
        c = 2 * z + 1 - y
        if s % 2 == 0:
            def one():
                arrive(s, c, pieces - 1)
                along(act, s, c, pieces - 1, True, True)
                act(hop(PAIR, s, c, pieces - 1))
            if_(turned(s, 1 - y), one)

    def relay(s, d, act, arrive):
        def from_side(z0, up):
            c = 2 * z0 + y

            def one(k):
                j = nth(s, k)
                arrive(s, c, j)
                along(act, s, c, j, up, not up)
                if s % 2 == 1:
                    act(hop(ACROSS, s, c, j))
                else:
                    if_(jnp.logical_or(j < pieces - 1, jnp.logical_not(turned(s, y))), lambda: act(hop(ACROSS, s, c, j)))
                act(hop(PAIR, s, c, j))
            each(blocks(s, z0), one)
            if s % 2 == 0:
                def far_one():
                    arrive(s, c + 1 - 2 * y, pieces - 1)
                    along(act, s, c + 1 - 2 * y, pieces - 1, up, not up)
                    act(hop(PAIR, s, c + 1 - 2 * y, pieces - 1))
                if_(turned(s, 1 - y), far_one)
        sides(d, from_side)

    def far(s, z0, act, arrive):
        c = 2 * z0 + 1 - y

        def one(k):
            arrive(s, c, k)
            act(hop(PAIR, s, c, k))
        if s % 2 == 0:
            each(pieces - jnp.where(turned(s, 1 - y), 1, 0), one)
        else:
            each(blocks(s, z0), one)

    def whole(s, z0):
        def wait(c):
            each(blocks(s, z0), lambda j: paired(s, c, j).wait_recv())
        if_(z0 != z, lambda: wait(2 * z0 + y))
        wait(2 * z0 + 1 - y)

    def span_of(i):
        return pl.ds(i * plane if isinstance(i, int) else pl.multiple_of(i * plane, plane), plane)

    def handed(i):
        return pltpu.make_async_remote_copy(
            src_ref=last.at[span_of(i), :], dst_ref=prior.at[span_of(i), :],
            send_sem=prior_send.at[i], recv_sem=prior_recv.at[i],
            device_id={"tm": section + 2}, device_id_type=MESH)

    def stored(l, i):
        return pltpu.make_async_copy(
            solved.at[l, span_of(i), :], out_ref.at[0, span_of(i), half_of(core)], store_sem.at[i])

    def passed(l, i):
        return pltpu.make_async_remote_copy(
            src_ref=solved.at[l, span_of(i), :], dst_ref=out_ref.at[0, span_of(i), half_of(core)],
            send_sem=out_send.at[i], recv_sem=out_recv.at[i], device_id=sibling, device_id_type=MESH)

    def couple(l, i):
        span = span_of(i)
        coupled = jnp.dot(factors[2 * l, span, :], (prior, middle)[l][...], preferred_element_type=jnp.float32)
        update[span, :] = (rhs[l, span, :].astype(jnp.float32) - coupled).astype(jnp.bfloat16)

    def solve(l, z0):
        def one(i):
            span = span_of(i)
            known = ((i * plane) // WIDE + 1) * WIDE
            result = jnp.dot(factors[2 * l + 1, span, :known], update[:known, :], preferred_element_type=jnp.float32)
            (middle, last)[l][span, :] = result.astype(jnp.bfloat16)
            if l == 1:
                if_(stage < stages - 1, lambda: handed(i).start())
            solved[l, span, :] = result
            if_(core == l, lambda: stored(l, i).start())
            if_(core != l, lambda: passed(l, i).start())
        if isinstance(z0, int):
            one(z0)
        else:
            for i in range(lines):
                if_(z0 == i, lambda i=i: one(i))

    start = lambda copy: copy.start()
    arrived = lambda s, c, j: hop(ACROSS, s, c, j).wait_recv()

    def ready(s):
        l, arr = divmod(s, 2)
        if_(core == l, lambda: own(arr).wait())
        if_(core != l, lambda: given(arr, 1 - core).wait_recv())

    def begin(s):
        ready(s)
        own_sends(s, start)
        turn(s, start, arrived)

    def work(s, z0):
        far(s, z0, start, arrived)

        @pl.when(stage == 0)
        def _():
            whole(s, z0)
            (couple, solve)[s % 2](s // 2, z0)

    begin(0)
    own_rhs.wait()
    given_rhs(1 - core).wait_recv()
    if_(stage == 0, own_carry.wait)
    for s in range(4):
        def step(d, carry, s=s):
            relay(s, d, start, arrived)

            def side(k, carry):
                z0 = jnp.where(k == 0, z - d + 1, z + d - 1)
                if_(jnp.logical_and(jnp.logical_and(z0 >= 0, z0 < lines), jnp.logical_or(d > 1, k == 0)), lambda: work(s, z0))
                return carry
            lax.fori_loop(0, 2, side, 0)

            @pl.when(d == lines - 1)
            def _():
                if s < 3:
                    begin(s + 1)

            return carry
        lax.fori_loop(1, lines, step, 0)

        def end(k, carry, s=s):
            z0 = jnp.where(k == 0, z - lines + 1, z + lines - 1)
            if_(jnp.logical_and(z0 >= 0, z0 < lines), lambda: work(s, z0))
            return carry
        lax.fori_loop(0, 2, end, 0)

    @pl.when(stage > 0)
    def _():
        def all_whole(s):
            each(lines, lambda z0: whole(s, z0))

        def add(k):
            handed(k).wait_recv()
            group = pl.ds(pl.multiple_of(k * plane, plane), plane)
            for i in range(pieces):
                span = pl.ds(i * WIDE, WIDE)
                solved[1, span, :] -= jnp.dot(factors[0, span, group], prior[group, :], preferred_element_type=jnp.float32)

        for s in range(4):
            all_whole(s)
        solved[1] = rhs[0].astype(jnp.float32)

        def adds(d, carry):
            def side(k, carry):
                z0 = jnp.where(k == 0, z - d, z + d)
                if_(jnp.logical_and(jnp.logical_and(z0 >= 0, z0 < lines), jnp.logical_or(d > 0, k == 0)), lambda: add(z0))
                return carry
            return lax.fori_loop(0, 2, side, carry)
        lax.fori_loop(0, lines, adds, 0)
        update[...] = solved[1].astype(jnp.bfloat16)
        for i in range(lines):
            solve(0, i)
        for i in range(lines):
            couple(1, i)
        for i in range(lines):
            solve(1, i)

    sent = lambda copy: copy.wait_send()
    none = lambda *_: None
    for s in range(4):
        own_sends(s, sent)
        turn(s, sent, none)
        lax.fori_loop(1, lines, lambda d, carry, s=s: (relay(s, d, sent, none), carry)[1], 0)
        each(lines, lambda z0, s=s: far(s, z0, sent, none))
    for arr in range(2):
        given(arr, core).wait_send()
    given_rhs(core).wait_send()

    def finish(i):
        for l in range(2):
            if_(core == l, lambda l=l: stored(l, i).wait())
            if_(core != l, lambda l=l: passed(l, i).wait())
        if_(stage < stages - 1, lambda: handed(i).wait_send())
    each(lines, finish)


def shards(stages, cols, inv_diag, sub_diag, rhs, carry_in):
    order, samples = carry_in.shape
    half, lines, pieces = samples // 2, cols // 2, order // WIDE
    flops = 4 * order * order * samples
    return pl.pallas_call(
        functools.partial(kernel, stages, lines),
        out_shape=jax.ShapeDtypeStruct(rhs.shape, jnp.float32),
        in_specs=[pl.BlockSpec(memory_space=pl.ANY)] * 4,
        out_specs=pl.BlockSpec(memory_space=pl.ANY),
        scratch_shapes=[
            pltpu.VMEM((4, order, order), jnp.bfloat16),
            pltpu.VMEM((2, order, half), jnp.bfloat16),
            pltpu.VMEM((order, half), jnp.bfloat16),
            pltpu.VMEM((order, half), jnp.bfloat16),
            pltpu.VMEM((order, half), jnp.bfloat16),
            pltpu.VMEM((order, half), jnp.bfloat16),
            pltpu.VMEM((2, order, half), jnp.float32),
            pltpu.SemaphoreType.DMA((2,)),
            pltpu.SemaphoreType.DMA((3,)),
            pltpu.SemaphoreType.DMA((3,)),
            pltpu.SemaphoreType.DMA,
            pltpu.SemaphoreType.DMA,
            pltpu.SemaphoreType.DMA((4, 4, cols, pieces)),
            pltpu.SemaphoreType.DMA((4, cols, pieces)),
            pltpu.SemaphoreType.DMA((4, cols, pieces)),
            pltpu.SemaphoreType.DMA((lines,)),
            pltpu.SemaphoreType.DMA((lines,)),
            pltpu.SemaphoreType.DMA((lines,)),
            pltpu.SemaphoreType.DMA((lines,)),
            pltpu.SemaphoreType.DMA((lines,)),
        ],
        compiler_params=pltpu.CompilerParams(
            collective_id=0, has_side_effects=True, vmem_limit_bytes=60 * 1024 * 1024),
        cost_estimate=pl.CostEstimate(flops=flops, bytes_accessed=10 * order * samples, transcendentals=0),
    )(inv_diag, sub_diag, rhs, carry_in)


def solution(mesh):
    in_specs = (
        P("tm", "cols", None),
        P("tm", "cols", None),
        P("tm", None, "cols"),
        P(None, "cols"),
    )
    out_specs = P("tm", None, "cols")
    body = functools.partial(shards, mesh.shape["tm"] // 2, mesh.shape["cols"])
    return jax.shard_map(body, mesh=mesh, in_specs=in_specs, out_specs=out_specs, check_vma=False)
```

```python
import functools

import jax
import jax.numpy as jnp
from jax import lax
from jax.experimental import pallas as pl
from jax.experimental.pallas import tpu as pltpu
from jax.sharding import PartitionSpec as P

MESH = pl.DeviceIdType.MESH
WIDE = 512
UP, DOWN, ACROSS, PAIR = 0, 1, 2, 3
LAG = 3
LAGM = 4
LATE = 7
LATER = 1


def kernel(stages, lines, inv_ref, sub_ref, rhs_ref, carry_ref, out_ref,
           factors, rhs, prior, update, staged,
           own_sem, give_send, give_recv, rhs_sem, carry_sem,
           send_sem, recv_sem, pair_sem, store_sem, out_send, out_recv, prior_send, prior_recv):
    section = lax.axis_index("tm")
    col = lax.axis_index("cols")
    stage, core = section // 2, lax.rem(section, 2)
    z, y = col // 2, lax.rem(col, 2)
    rows, order = inv_ref.shape[1], inv_ref.shape[2]
    half = rhs_ref.shape[2] // 2
    plane, pieces = 2 * rows, order // WIDE
    narrow = WIDE // 2
    sibling = {"tm": 2 * stage + 1 - core}

    def if_(cond, fn):
        pl.when(cond)(fn)

    def each(count, fn):
        def body(j, carry):
            fn(j)
            return carry
        lax.fori_loop(0, count, body, 0)

    mine = pl.ds(pl.multiple_of(col * rows, rows), rows)

    def own(arr):
        return pltpu.make_async_copy((sub_ref, inv_ref)[arr].at[0], factors.at[2 * core + arr, mine, :], own_sem.at[arr])

    def given(arr, owner):
        return pltpu.make_async_remote_copy(
            src_ref=(sub_ref, inv_ref)[arr].at[0], dst_ref=factors.at[2 * owner + arr, mine, :],
            send_sem=give_send.at[arr], recv_sem=give_recv.at[arr], device_id=sibling, device_id_type=MESH)

    def half_of(c):
        return pl.ds(pl.multiple_of(c * half, half), half)

    own_rhs = pltpu.make_async_copy(rhs_ref.at[0, :, half_of(core)], rhs.at[core], rhs_sem)

    def given_rhs(owner):
        return pltpu.make_async_remote_copy(
            src_ref=rhs_ref.at[0, :, half_of(1 - core)], dst_ref=rhs.at[owner],
            send_sem=give_send.at[2], recv_sem=give_recv.at[2], device_id=sibling, device_id_type=MESH)

    own_carry = pltpu.make_async_copy(carry_ref.at[:, half_of(core)], prior.at[0], carry_sem)

    own(0).start()
    own(1).start()

    barrier = pltpu.get_barrier_semaphore()

    def greet(cond, device):
        @pl.when(cond)
        def _():
            pl.semaphore_signal(barrier, inc=1, device_id=device, device_id_type=MESH)

    greet(z > 0, {"cols": col - 2})
    greet(z < lines - 1, {"cols": col + 2})
    pl.semaphore_signal(barrier, inc=1, device_id={"cols": 2 * z + 1 - y}, device_id_type=MESH)
    pl.semaphore_signal(barrier, inc=1, device_id=sibling, device_id_type=MESH)
    greet(stage > 0, {"tm": section - 2})
    greet(stage < stages - 1, {"tm": section + 2})
    ends = [z > 0, z < lines - 1, stage > 0, stage < stages - 1]
    pl.semaphore_wait(barrier, 2 + sum(jnp.where(end, 1, 0) for end in ends))

    given(0, core).start()
    given(1, core).start()
    own_rhs.start()
    given_rhs(core).start()
    if_(stage == 0, own_carry.start)

    first = stage == 0

    def even(s):
        return lax.rem(s, 2) == 0

    def blocks(s, c):
        return jnp.where(even(s), pieces, (c * rows) // WIDE + 1)

    def turns(s, c):
        return jnp.where(s == 0, 1, jnp.where(s == 2, lax.rem(c, 2), 0))

    def nth(s, c, k):
        return lax.rem(k + blocks(s, c) - turns(s, c), blocks(s, c))

    def hop(way, s, c, j, wide):
        ref = factors.at[s, pl.ds(pl.multiple_of(c * rows, rows), rows), pl.ds(pl.multiple_of(j * WIDE, WIDE), wide)]
        to = ({"tm": 2 * stage, "cols": col + 2}, {"tm": 2 * stage + 1, "cols": col - 2}, {"cols": 2 * z + 1 - y}, sibling)[way]
        return pltpu.make_async_remote_copy(
            src_ref=ref, dst_ref=ref, send_sem=send_sem.at[way, s, c, j],
            recv_sem=pair_sem.at[s, c, j] if way == PAIR else recv_sem.at[s, c, j], device_id=to, device_id_type=MESH)

    def mine_of(z0, j):
        return jnp.where(z0 == z, lax.rem(j, 2) == core, (core == 0) == (z0 < z))

    def cut(s, c, j):
        return jnp.logical_and(jnp.logical_not(even(s)), (c + 1) * rows <= j * WIDE + narrow)

    def by_width(s, c, j, fn):
        short = cut(s, c, j)
        if_(short, lambda: fn(narrow))
        if_(jnp.logical_not(short), lambda: fn(WIDE))

    def moves(act, s, c, j, up, down, across, pair, arrive):
        def fn(wide):
            if arrive:
                hop(ACROSS, s, c, j, wide).wait_recv()
            for way, cond in ((UP, up), (DOWN, down), (ACROSS, across), (PAIR, pair)):
                if cond is True:
                    act(hop(way, s, c, j, wide))
                elif cond is not False:
                    if_(cond, lambda way=way: act(hop(way, s, c, j, wide)))
        by_width(s, c, j, fn)

    can_up, can_down = z < lines - 1, z > 0
    up, down = jnp.logical_and(can_up, core == 0), jnp.logical_and(can_down, core == 1)

    def own_sends(s, act):
        def one(k):
            j = nth(s, col, k)
            across = jnp.logical_and(k >= turns(s, col), lax.rem(j, 2) == core)
            moves(act, s, col, j, up, down, across, False, False)
        each(blocks(s, col), one)

    def turning(act):
        def of(s):
            def one(k):
                j = nth(s, col, k)
                if_(lax.rem(j, 2) == core, lambda: moves(act, s, col, j, False, False, True, False, False))
            each(turns(s, col), one)
        each(4, of)

    def turn(s, act, arrive):
        c = 2 * z + 1 - y

        def one(k):
            j = nth(s, c, k)
            if_(lax.rem(j, 2) == core, lambda: moves(act, s, c, j, can_up, can_down, False, True, arrive))
        each(turns(s, c), one)

    def relay(s, d, act, arrive):
        z0 = jnp.where(core == 0, z - d, z + d)

        @pl.when(jnp.logical_and(z0 >= 0, z0 < lines))
        def _():
            near, across_from = 2 * z0 + y, 2 * z0 + 1 - y
            count = blocks(s, near)

            def one(i):
                is_far = i >= count
                c = jnp.where(is_far, across_from, near)
                j = nth(s, c, jnp.where(is_far, i - count, i))
                across = jnp.logical_and(jnp.logical_not(is_far), j < count - turns(s, near))
                moves(act, s, c, j, up, down, across, True, arrive)
            each(count + turns(s, across_from), one)

    def far(s, z0, act, arrive):
        c = 2 * z0 + 1 - y

        def one(j):
            if_(mine_of(z0, j), lambda: moves(act, s, c, j, False, False, False, True, arrive))
        each(blocks(s, c) - turns(s, c), one)

    def whole(s, z0):
        def wait(c):
            def one(j):
                if_(jnp.logical_not(mine_of(z0, j)), lambda: by_width(s, c, j, lambda wide: hop(PAIR, s, c, j, wide).wait_recv()))
            each(blocks(s, c), one)
        if_(z0 != z, lambda: wait(2 * z0 + y))
        wait(2 * z0 + 1 - y)

    def span_of(c):
        return pl.ds(c * rows if isinstance(c, int) else pl.multiple_of(c * rows, rows), rows)

    def handed(c):
        return pltpu.make_async_remote_copy(
            src_ref=prior.at[2, span_of(c), :], dst_ref=prior.at[0, span_of(c), :],
            send_sem=prior_send.at[c], recv_sem=prior_recv.at[c],
            device_id={"tm": section + 2}, device_id_type=MESH)

    def stored(l, c):
        return pltpu.make_async_copy(
            staged.at[l, span_of(c), :], out_ref.at[0, span_of(c), half_of(core)], store_sem.at[c])

    def passed(l, c, owner):
        return pltpu.make_async_remote_copy(
            src_ref=staged.at[l, span_of(c), :], dst_ref=out_ref.at[0, span_of(c), half_of(owner)],
            send_sem=out_send.at[c], recv_sem=out_recv.at[c], device_id=sibling, device_id_type=MESH)

    def couple(l, z0):
        span = pl.ds(pl.multiple_of(z0 * plane, plane), plane)
        coupled = jnp.dot(factors[2 * l, span, :], prior[l], preferred_element_type=jnp.float32)
        update[span, :] = (rhs[l, span, :].astype(jnp.float32) - coupled).astype(jnp.bfloat16)

    def solve(l, c):
        for i in range(2 * lines):
            @pl.when(c == i)
            def _(i=i):
                known = -(-(i + 1) * rows // narrow) * narrow
                result = jnp.dot(factors[2 * l + 1, span_of(i), :known], update[:known, :], preferred_element_type=jnp.float32)
                prior[l + 1, span_of(i), :] = result.astype(jnp.bfloat16)
                if_(jnp.logical_and(l == 1, stage < stages - 1), lambda: handed(i).start())
                staged[l, span_of(i), :] = result
                if_(core == l, lambda: stored(l, i).start())
                if_(core != l, lambda: passed(l, i, core).start())

    start = lambda copy: copy.start()

    def ready(s):
        l, arr = s // 2, lax.rem(s, 2)
        for a in range(2):
            if_(jnp.logical_and(core == l, arr == a), lambda a=a: own(a).wait())
            if_(jnp.logical_and(core != l, arr == a), lambda a=a: given(a, 1 - core).wait_recv())

    def fetch(s, z0):
        far(s, z0, start, True)

    def work(s, z0):
        @pl.when(first)
        def _():
            whole(s, z0)
            if_(even(s), lambda: couple(s // 2, z0))

            @pl.when(jnp.logical_not(even(s)))
            def _():
                lax.fori_loop(0, 2, lambda k, carry: (solve(s // 2, 2 * z0 + k), carry)[1], 0)

    each(4, ready)
    turning(start)
    own_sends(0, start)
    own_rhs.wait()
    given_rhs(1 - core).wait_recv()
    if_(first, own_carry.wait)

    steps = 4 * lines

    def in_order(d, fn):
        def side(k, carry):
            z0 = jnp.where(k == 0, z - d, z + d)
            if_(jnp.logical_and(jnp.logical_and(z0 >= 0, z0 < lines), jnp.logical_or(d > 0, k == 0)), lambda: fn(z0))
            return carry
        lax.fori_loop(0, 2, side, 0)

    def items(t, lag, fn):
        w = t - lag
        if_(jnp.logical_and(w >= 0, w < steps), lambda: in_order(lax.rem(w, lines), lambda z0: fn(w // lines, z0)))

    inside = jnp.logical_and(z > 0, z < lines - 1)
    lag = jnp.where(first, jnp.where(inside, LAGM, LAG), LATE)

    def step(t, carry):
        s, d = t // lines, lax.rem(t, lines)

        @pl.when(t < steps)
        def _():
            if_(d == 0, lambda: turn(s, start, True))
            if_(d > 0, lambda: relay(s, d, start, True))
            if_(jnp.logical_and(d == lines - 1, s < 3), lambda: own_sends(s + 1, start))
        items(t, lag, fetch)
        items(t, lag + LATER, work)
        return carry
    lax.fori_loop(0, steps + max(LAG, LAGM, LATE) + LATER, step, 0)

    @pl.when(stage > 0)
    def _():
        each(4, lambda s: each(lines, lambda z0: whole(s, z0)))
        staged[1] = rhs[0].astype(jnp.float32)

        def add(k):
            for c in range(2):
                handed(2 * k + c).wait_recv()
            group = pl.ds(pl.multiple_of(k * plane, plane), plane)
            for i in range(pieces):
                span = pl.ds(i * WIDE, WIDE)
                staged[1, span, :] -= jnp.dot(factors[0, span, group], prior[0, group, :], preferred_element_type=jnp.float32)
        each(lines, lambda d: in_order(d, add))
        update[...] = staged[1].astype(jnp.bfloat16)
        each(2 * lines, lambda c: solve(0, c))
        each(lines, lambda z0: couple(1, z0))
        each(2 * lines, lambda c: solve(1, c))

    sent = lambda copy: copy.wait_send()

    turning(sent)

    def sends(s):
        own_sends(s, sent)
        turn(s, sent, False)
        lax.fori_loop(1, lines, lambda d, carry: (relay(s, d, sent, False), carry)[1], 0)
        each(lines, lambda z0: far(s, z0, sent, False))
    each(4, sends)
    for arr in range(2):
        given(arr, core).wait_send()
    given_rhs(core).wait_send()

    def finish(c):
        for l in range(2):
            if_(core == l, lambda l=l: stored(l, c).wait())
            if_(core != l, lambda l=l: passed(l, c, core).wait_send())
        passed(0, c, 1 - core).wait_recv()
        if_(stage < stages - 1, lambda: handed(c).wait_send())
    each(2 * lines, finish)


def shards(stages, cols, inv_diag, sub_diag, rhs, carry_in):
    order, samples = carry_in.shape
    half, lines, pieces = samples // 2, cols // 2, order // WIDE
    flops = 4 * order * order * samples
    return pl.pallas_call(
        functools.partial(kernel, stages, lines),
        out_shape=jax.ShapeDtypeStruct(rhs.shape, jnp.float32),
        in_specs=[pl.BlockSpec(memory_space=pl.ANY)] * 4,
        out_specs=pl.BlockSpec(memory_space=pl.ANY),
        scratch_shapes=[
            pltpu.VMEM((4, order, order), jnp.bfloat16),
            pltpu.VMEM((2, order, half), jnp.bfloat16),
            pltpu.VMEM((3, order, half), jnp.bfloat16),
            pltpu.VMEM((order, half), jnp.bfloat16),
            pltpu.VMEM((2, order, half), jnp.float32),
            pltpu.SemaphoreType.DMA((2,)),
            pltpu.SemaphoreType.DMA((3,)),
            pltpu.SemaphoreType.DMA((3,)),
            pltpu.SemaphoreType.DMA,
            pltpu.SemaphoreType.DMA,
            pltpu.SemaphoreType.DMA((4, 4, cols, pieces)),
            pltpu.SemaphoreType.DMA((4, cols, pieces)),
            pltpu.SemaphoreType.DMA((4, cols, pieces)),
            pltpu.SemaphoreType.DMA((cols,)),
            pltpu.SemaphoreType.DMA((cols,)),
            pltpu.SemaphoreType.DMA((cols,)),
            pltpu.SemaphoreType.DMA((cols,)),
            pltpu.SemaphoreType.DMA((cols,)),
        ],
        compiler_params=pltpu.CompilerParams(
            collective_id=0, has_side_effects=True, vmem_limit_bytes=60 * 1024 * 1024),
        cost_estimate=pl.CostEstimate(flops=flops, bytes_accessed=10 * order * samples, transcendentals=0),
    )(inv_diag, sub_diag, rhs, carry_in)


def solution(mesh):
    in_specs = (
        P("tm", "cols", None),
        P("tm", "cols", None),
        P("tm", None, "cols"),
        P(None, "cols"),
    )
    out_specs = P("tm", None, "cols")
    body = functools.partial(shards, mesh.shape["tm"] // 2, mesh.shape["cols"])
    return jax.shard_map(body, mesh=mesh, in_specs=in_specs, out_specs=out_specs, check_vma=False)
```

```python
import functools

import jax
import jax.numpy as jnp
from jax import lax
from jax.experimental import pallas as pl
from jax.experimental.pallas import tpu as pltpu
from jax.sharding import PartitionSpec as P

MESH = pl.DeviceIdType.MESH
WIDE = 512
UP, DOWN, ACROSS, PAIR = 0, 1, 2, 3
LAG = 4
LAGM = 4
LATE = 6
AHEAD = 2
LAST = 2
END_LAG = 1
BEHIND = 1
TALL = 1024


def kernel(stages, lines, inv_ref, sub_ref, rhs_ref, carry_ref, out_ref,
           factors, rhs, prior, update, staged,
           own_sem, give_send, give_recv, rhs_sem, carry_sem,
           send_sem, recv_sem, pair_sem, store_sem, out_send, out_recv, prior_send, prior_recv):
    section = lax.axis_index("tm")
    col = lax.axis_index("cols")
    stage, core = section // 2, lax.rem(section, 2)
    z, y = col // 2, lax.rem(col, 2)
    rows, order = inv_ref.shape[1], inv_ref.shape[2]
    half = rhs_ref.shape[2] // 2
    plane, pieces = 2 * rows, order // WIDE
    narrow = WIDE // 2
    sibling = {"tm": 2 * stage + 1 - core}

    def if_(cond, fn):
        pl.when(cond)(fn)

    def each(count, fn):
        def body(j, carry):
            fn(j)
            return carry
        lax.fori_loop(0, count, body, 0)

    mine = pl.ds(pl.multiple_of(col * rows, rows), rows)

    def own(arr):
        return pltpu.make_async_copy((sub_ref, inv_ref)[arr].at[0], factors.at[2 * core + arr, mine, :], own_sem.at[arr])

    def given(arr, owner):
        return pltpu.make_async_remote_copy(
            src_ref=(sub_ref, inv_ref)[arr].at[0], dst_ref=factors.at[2 * owner + arr, mine, :],
            send_sem=give_send.at[arr], recv_sem=give_recv.at[arr], device_id=sibling, device_id_type=MESH)

    def half_of(c):
        return pl.ds(pl.multiple_of(c * half, half), half)

    own_rhs = pltpu.make_async_copy(rhs_ref.at[0, :, half_of(core)], rhs.at[core], rhs_sem)

    def given_rhs(owner):
        return pltpu.make_async_remote_copy(
            src_ref=rhs_ref.at[0, :, half_of(1 - core)], dst_ref=rhs.at[owner],
            send_sem=give_send.at[2], recv_sem=give_recv.at[2], device_id=sibling, device_id_type=MESH)

    own_carry = pltpu.make_async_copy(carry_ref.at[:, half_of(core)], prior.at[0], carry_sem)

    own(0).start()
    own(1).start()

    barrier = pltpu.get_barrier_semaphore()

    def greet(cond, device):
        @pl.when(cond)
        def _():
            pl.semaphore_signal(barrier, inc=1, device_id=device, device_id_type=MESH)

    greet(z > 0, {"cols": col - 2})
    greet(z < lines - 1, {"cols": col + 2})
    pl.semaphore_signal(barrier, inc=1, device_id={"cols": 2 * z + 1 - y}, device_id_type=MESH)
    pl.semaphore_signal(barrier, inc=1, device_id=sibling, device_id_type=MESH)
    greet(stage > 0, {"tm": section - 2})
    greet(stage < stages - 1, {"tm": section + 2})
    ends = [z > 0, z < lines - 1, stage > 0, stage < stages - 1]
    pl.semaphore_wait(barrier, 2 + sum(jnp.where(end, 1, 0) for end in ends))

    given(0, core).start()

    first = stage == 0

    def even(s):
        return lax.rem(s, 2) == 0

    def blocks(s, c):
        return jnp.where(even(s), pieces, (c * rows) // WIDE + 1)

    def turns(s, c):
        return jnp.where(s == 0, 1, jnp.where(s == 2, lax.rem(c, 2), 0))

    def nth(s, c, k):
        return lax.rem(k + blocks(s, c) - turns(s, c), blocks(s, c))

    def hop(way, s, c, j, wide):
        ref = factors.at[s, pl.ds(pl.multiple_of(c * rows, rows), rows), pl.ds(pl.multiple_of(j * WIDE, WIDE), wide)]
        to = ({"tm": 2 * stage, "cols": col + 2}, {"tm": 2 * stage + 1, "cols": col - 2}, {"cols": 2 * z + 1 - y}, sibling)[way]
        return pltpu.make_async_remote_copy(
            src_ref=ref, dst_ref=ref, send_sem=send_sem.at[way, s, c, j],
            recv_sem=pair_sem.at[s, c, j] if way == PAIR else recv_sem.at[s, c, j], device_id=to, device_id_type=MESH)

    light = core == jnp.where(2 * z < lines, 0, 1)

    def mine_of(z0):
        return jnp.where(z0 == z, light, (core == 0) == (z0 < z))

    def cut(s, c, j):
        return jnp.logical_and(jnp.logical_not(even(s)), (c + 1) * rows <= j * WIDE + narrow)

    def by_width(s, c, j, fn):
        short = cut(s, c, j)
        if_(short, lambda: fn(narrow))
        if_(jnp.logical_not(short), lambda: fn(WIDE))

    def moves(act, s, c, j, up, down, across, pair, arrive):
        def fn(wide):
            if arrive:
                hop(ACROSS, s, c, j, wide).wait_recv()
            for way, cond in ((UP, up), (DOWN, down), (ACROSS, across), (PAIR, pair)):
                if cond is True:
                    act(hop(way, s, c, j, wide))
                elif cond is not False:
                    if_(cond, lambda way=way: act(hop(way, s, c, j, wide)))
        by_width(s, c, j, fn)

    can_up, can_down = z < lines - 1, z > 0
    up, down = jnp.logical_and(can_up, core == 0), jnp.logical_and(can_down, core == 1)

    def own_sends(s, act):
        def one(k):
            j = nth(s, col, k)
            across = jnp.logical_and(k >= turns(s, col), light)
            moves(act, s, col, j, up, down, across, False, False)
        each(blocks(s, col), one)

    def turning(act):
        def of(s):
            if_(light, lambda: each(turns(s, col), lambda k: moves(act, s, col, nth(s, col, k), False, False, True, False, False)))
        return of

    def turn(s, act, arrive):
        c = 2 * z + 1 - y

        if_(light, lambda: each(turns(s, c), lambda k: moves(act, s, c, nth(s, c, k), can_up, can_down, False, True, arrive)))

    def relay(s, d, act, arrive):
        z0 = jnp.where(core == 0, z - d, z + d)

        @pl.when(jnp.logical_and(z0 >= 0, z0 < lines))
        def _():
            near, across_from = 2 * z0 + y, 2 * z0 + 1 - y
            count = blocks(s, near)

            def one(i):
                is_far = i >= count
                c = jnp.where(is_far, across_from, near)
                j = nth(s, c, jnp.where(is_far, i - count, i))
                across = jnp.logical_and(jnp.logical_not(is_far), j < count - turns(s, near))
                moves(act, s, c, j, up, down, across, True, arrive)
            each(count + turns(s, across_from), one)

    def far(s, z0, act, arrive):
        c = 2 * z0 + 1 - y

        def one(j):
            if_(mine_of(z0), lambda: moves(act, s, c, j, False, False, False, True, arrive))
        each(blocks(s, c) - turns(s, c), one)

    def whole(s, z0):
        def wait(c):
            def one(j):
                if_(jnp.logical_not(mine_of(z0)), lambda: by_width(s, c, j, lambda wide: hop(PAIR, s, c, j, wide).wait_recv()))
            each(blocks(s, c), one)
        if_(z0 != z, lambda: wait(2 * z0 + y))
        wait(2 * z0 + 1 - y)

    def span_of(c):
        return pl.ds(c * rows if isinstance(c, int) else pl.multiple_of(c * rows, rows), rows)

    def handed(c):
        return pltpu.make_async_remote_copy(
            src_ref=prior.at[2, span_of(c), :], dst_ref=prior.at[0, span_of(c), :],
            send_sem=prior_send.at[c], recv_sem=prior_recv.at[c],
            device_id={"tm": section + 2}, device_id_type=MESH)

    def stored(l, c):
        return pltpu.make_async_copy(
            prior.at[l + 1, span_of(c), :], out_ref.at[0, span_of(c), half_of(core)], store_sem.at[c])

    def passed(l, c, owner):
        return pltpu.make_async_remote_copy(
            src_ref=prior.at[l + 1, span_of(c), :], dst_ref=out_ref.at[0, span_of(c), half_of(owner)],
            send_sem=out_send.at[c], recv_sem=out_recv.at[c], device_id=sibling, device_id_type=MESH)

    def couple(l, z0):
        span = pl.ds(pl.multiple_of(z0 * plane, plane), plane)
        coupled = jnp.dot(factors[2 * l, span, :], prior[l], preferred_element_type=jnp.float32)
        update[span, :] = (rhs[l, span, :].astype(jnp.float32) - coupled).astype(jnp.bfloat16)

    def solve(l, z0):
        for i in range(lines):
            @pl.when(z0 == i)
            def _(i=i):
                both, lower = slice(i * plane, (i + 1) * plane), slice(i * plane + rows, (i + 1) * plane)
                known, rest = (-(-(2 * i + k) * rows // narrow) * narrow for k in (1, 2))
                result = jnp.dot(factors[2 * l + 1, both, :known], update[:known, :], preferred_element_type=jnp.float32)
                if rest > known:
                    more = jnp.dot(factors[2 * l + 1, lower, known:rest], update[known:rest, :], preferred_element_type=jnp.float32)
                    prior[l + 1, slice(i * plane, i * plane + rows), :] = result[:rows].astype(jnp.bfloat16)
                    prior[l + 1, lower, :] = (result[rows:] + more).astype(jnp.bfloat16)
                else:
                    prior[l + 1, both, :] = result.astype(jnp.bfloat16)
                for c in (2 * i, 2 * i + 1):
                    if_(jnp.logical_and(l == 1, stage < stages - 1), lambda c=c: handed(c).start())
                for c in (2 * i, 2 * i + 1):
                    if_(core == l, lambda c=c: stored(l, c).start())
                    if_(core != l, lambda c=c: passed(l, c, core).start())

    start = lambda copy: copy.start()

    def ready(s):
        l, arr = s // 2, lax.rem(s, 2)
        for a in range(2):
            if_(jnp.logical_and(core == l, arr == a), lambda a=a: own(a).wait())
            if_(jnp.logical_and(core != l, arr == a), lambda a=a: given(a, 1 - core).wait_recv())

    def fetch(s, z0):
        far(s, z0, start, True)

    def work(s, z0):
        @pl.when(first)
        def _():
            whole(s, z0)
            if_(even(s), lambda: couple(s // 2, z0))

            @pl.when(jnp.logical_not(even(s)))
            def _():
                solve(s // 2, z0)

    ready(0)
    turning(start)(0)
    own_sends(0, start)
    given(1, core).start()
    if_(first, own_carry.start)
    own_rhs.start()
    given_rhs(core).start()
    ready(2)
    turning(start)(2)
    ready(1)
    ready(3)
    own_rhs.wait()
    given_rhs(1 - core).wait_recv()
    if_(first, own_carry.wait)

    steps = 4 * lines

    def in_order(d, fn):
        def side(k, carry):
            z0 = jnp.where(k == 0, z - d, z + d)
            if_(jnp.logical_and(jnp.logical_and(z0 >= 0, z0 < lines), jnp.logical_or(d > 0, k == 0)), lambda: fn(z0))
            return carry
        lax.fori_loop(0, 2, side, 0)

    inside = jnp.logical_and(z > 0, z < lines - 1)
    lag = jnp.where(first, jnp.where(inside, LAGM, LAG), LATE)
    ending = jnp.where(jnp.logical_and(first, jnp.logical_not(inside)), steps - lines + LAST, steps + 99)

    def due(t):
        late = jnp.where(t >= ending, END_LAG, lag)
        return jnp.clip(2 * (t - late), 0, 2 * steps + BEHIND)

    def half_step(h, fn):
        w, k = h // 2, lax.rem(h, 2)
        s, d = w // lines, lax.rem(w, lines)
        z0 = jnp.where(k == 0, z - d, z + d)
        real = jnp.logical_and(jnp.logical_and(h >= 0, h < 2 * steps), jnp.logical_or(d > 0, k == 0))
        if_(jnp.logical_and(real, jnp.logical_and(z0 >= 0, z0 < lines)), lambda: fn(s, z0))

    def step(t, carry):
        s, d = t // lines, lax.rem(t, lines)

        @pl.when(t < steps)
        def _():
            if_(d == 0, lambda: turn(s, start, True))
            if_(d > 0, lambda: relay(s, d, start, True))
            if_(jnp.logical_and(d == lines - AHEAD, s < 3), lambda: own_sends(s + 1, start))

        def item(h, carry):
            half_step(h, fetch)
            half_step(h - BEHIND, work)
            return carry
        lax.fori_loop(due(t), due(t + 1), item, 0)
        return carry
    lax.fori_loop(0, steps + max(LAG, LAGM, LATE) + BEHIND, step, 0)

    @pl.when(stage > 0)
    def _():
        each(4, lambda s: each(lines, lambda z0: whole(s, z0)))
        staged[...] = rhs[0].astype(jnp.float32)

        def add(k):
            for c in range(2):
                handed(2 * k + c).wait_recv()
            group = pl.ds(pl.multiple_of(k * plane, plane), plane)
            for i in range(pieces):
                span = pl.ds(i * WIDE, WIDE)
                staged[span, :] -= jnp.dot(factors[0, span, group], prior[0, group, :], preferred_element_type=jnp.float32)
        each(lines, lambda d: in_order(d, add))
        update[...] = staged[...].astype(jnp.bfloat16)
        each(lines, lambda z0: solve(0, z0))
        for i in range(order // TALL):
            span = slice(i * TALL, (i + 1) * TALL)
            coupled = jnp.dot(factors[2, span, :], prior[1], preferred_element_type=jnp.float32)
            update[span, :] = (rhs[1, span, :].astype(jnp.float32) - coupled).astype(jnp.bfloat16)
        each(lines, lambda z0: solve(1, z0))

    sent = lambda copy: copy.wait_send()

    each(4, turning(sent))

    def sends(s):
        own_sends(s, sent)
        turn(s, sent, False)
        lax.fori_loop(1, lines, lambda d, carry: (relay(s, d, sent, False), carry)[1], 0)
        each(lines, lambda z0: far(s, z0, sent, False))
    each(4, sends)
    for arr in range(2):
        given(arr, core).wait_send()
    given_rhs(core).wait_send()

    def finish(c):
        for l in range(2):
            if_(core == l, lambda l=l: stored(l, c).wait())
            if_(core != l, lambda l=l: passed(l, c, core).wait_send())
        passed(0, c, 1 - core).wait_recv()
        if_(stage < stages - 1, lambda: handed(c).wait_send())
    each(2 * lines, finish)


def shards(stages, cols, inv_diag, sub_diag, rhs, carry_in):
    order, samples = carry_in.shape
    half, lines, pieces = samples // 2, cols // 2, order // WIDE
    flops = 4 * order * order * samples
    return pl.pallas_call(
        functools.partial(kernel, stages, lines),
        out_shape=jax.ShapeDtypeStruct(rhs.shape, jnp.bfloat16),
        in_specs=[pl.BlockSpec(memory_space=pl.ANY)] * 4,
        out_specs=pl.BlockSpec(memory_space=pl.ANY),
        scratch_shapes=[
            pltpu.VMEM((4, order, order), jnp.bfloat16),
            pltpu.VMEM((2, order, half), jnp.bfloat16),
            pltpu.VMEM((3, order, half), jnp.bfloat16),
            pltpu.VMEM((order, half), jnp.bfloat16),
            pltpu.VMEM((order, half), jnp.float32),
            pltpu.SemaphoreType.DMA((2,)),
            pltpu.SemaphoreType.DMA((3,)),
            pltpu.SemaphoreType.DMA((3,)),
            pltpu.SemaphoreType.DMA,
            pltpu.SemaphoreType.DMA,
            pltpu.SemaphoreType.DMA((4, 4, cols, pieces)),
            pltpu.SemaphoreType.DMA((4, cols, pieces)),
            pltpu.SemaphoreType.DMA((4, cols, pieces)),
            pltpu.SemaphoreType.DMA((cols,)),
            pltpu.SemaphoreType.DMA((cols,)),
            pltpu.SemaphoreType.DMA((cols,)),
            pltpu.SemaphoreType.DMA((cols,)),
            pltpu.SemaphoreType.DMA((cols,)),
        ],
        compiler_params=pltpu.CompilerParams(
            collective_id=0, has_side_effects=True, vmem_limit_bytes=60 * 1024 * 1024),
        cost_estimate=pl.CostEstimate(flops=flops, bytes_accessed=10 * order * samples, transcendentals=0),
    )(inv_diag, sub_diag, rhs, carry_in).astype(jnp.float32)


def solution(mesh):
    in_specs = (
        P("tm", "cols", None),
        P("tm", "cols", None),
        P("tm", None, "cols"),
        P(None, "cols"),
    )
    out_specs = P("tm", None, "cols")
    body = functools.partial(shards, mesh.shape["tm"] // 2, mesh.shape["cols"])
    return jax.shard_map(body, mesh=mesh, in_specs=in_specs, out_specs=out_specs, check_vma=False)
```

```python
import functools

import jax
import jax.numpy as jnp
from jax import lax
from jax.experimental import pallas as pl
from jax.experimental.pallas import tpu as pltpu
from jax.sharding import PartitionSpec as P

MESH = pl.DeviceIdType.MESH
WIDE = 512
UP, DOWN, ACROSS, PAIR = 0, 1, 2, 3
LAG = 4
LAGM = 4
LATE = 6
AHEAD = 2
LAST = 1
END_LAG = 1
BEHIND = 1
TALL = 1024
STEPS = 8
WIDEN_MIB = 60


def kernel(stages, lines, inv_ref, sub_ref, rhs_ref, carry_ref, out_ref,
           factors, rhs, prior, update, staged,
           own_sem, give_send, give_recv, rhs_sem, carry_sem,
           send_sem, recv_sem, pair_sem, store_sem, out_send, out_recv, prior_send, prior_recv):
    section = lax.axis_index("tm")
    col = lax.axis_index("cols")
    stage, core = section // 2, lax.rem(section, 2)
    z, y = col // 2, lax.rem(col, 2)
    rows, order = inv_ref.shape[1], inv_ref.shape[2]
    half = rhs_ref.shape[2] // 2
    plane, pieces = 2 * rows, order // WIDE
    narrow = WIDE // 2
    sibling = {"tm": 2 * stage + 1 - core}

    def if_(cond, fn):
        pl.when(cond)(fn)

    def each(count, fn):
        def body(j, carry):
            fn(j)
            return carry
        lax.fori_loop(0, count, body, 0)

    mine = pl.ds(pl.multiple_of(col * rows, rows), rows)

    def own(arr):
        return pltpu.make_async_copy((sub_ref, inv_ref)[arr].at[0], factors.at[2 * core + arr, mine, :], own_sem.at[arr])

    def given(arr, owner):
        return pltpu.make_async_remote_copy(
            src_ref=(sub_ref, inv_ref)[arr].at[0], dst_ref=factors.at[2 * owner + arr, mine, :],
            send_sem=give_send.at[arr], recv_sem=give_recv.at[arr], device_id=sibling, device_id_type=MESH)

    def half_of(c):
        return pl.ds(pl.multiple_of(c * half, half), half)

    own_rhs = pltpu.make_async_copy(rhs_ref.at[0, :, half_of(core)], rhs.at[core], rhs_sem)

    def given_rhs(owner):
        return pltpu.make_async_remote_copy(
            src_ref=rhs_ref.at[0, :, half_of(1 - core)], dst_ref=rhs.at[owner],
            send_sem=give_send.at[2], recv_sem=give_recv.at[2], device_id=sibling, device_id_type=MESH)

    own_carry = pltpu.make_async_copy(carry_ref.at[:, half_of(core)], prior.at[0], carry_sem)

    own(0).start()
    own(1).start()

    barrier = pltpu.get_barrier_semaphore()

    def greet(cond, device):
        @pl.when(cond)
        def _():
            pl.semaphore_signal(barrier, inc=1, device_id=device, device_id_type=MESH)

    greet(z > 0, {"cols": col - 2})
    greet(z < lines - 1, {"cols": col + 2})
    pl.semaphore_signal(barrier, inc=1, device_id={"cols": 2 * z + 1 - y}, device_id_type=MESH)
    pl.semaphore_signal(barrier, inc=1, device_id=sibling, device_id_type=MESH)
    greet(stage > 0, {"tm": section - 2})
    greet(stage < stages - 1, {"tm": section + 2})
    ends = [z > 0, z < lines - 1, stage > 0, stage < stages - 1]
    pl.semaphore_wait(barrier, 2 + sum(jnp.where(end, 1, 0) for end in ends))

    given(0, core).start()

    first = stage == 0

    def even(s):
        return lax.rem(s, 2) == 0

    def blocks(s, c):
        return jnp.where(even(s), pieces, (c * rows) // WIDE + 1)

    def turns(s, c):
        z0, y0 = c // 2, lax.rem(c, 2)
        third = jnp.where(z0 == 0, jnp.where(y0 == 1, pieces, 1), jnp.where(z0 == lines - 1, 0, y0))
        return jnp.where(s == 0, 1, jnp.where(s == 2, third, jnp.where(jnp.logical_and(s == 3, z0 == 0), 1, 0)))

    def nth(s, c, k):
        return lax.rem(k + blocks(s, c) - turns(s, c), blocks(s, c))

    def hop(way, s, c, j, wide):
        ref = factors.at[s, pl.ds(pl.multiple_of(c * rows, rows), rows), pl.ds(pl.multiple_of(j * WIDE, WIDE), wide)]
        to = ({"tm": 2 * stage, "cols": col + 2}, {"tm": 2 * stage + 1, "cols": col - 2}, {"cols": 2 * z + 1 - y}, sibling)[way]
        return pltpu.make_async_remote_copy(
            src_ref=ref, dst_ref=ref, send_sem=send_sem.at[way, s, c, j],
            recv_sem=pair_sem.at[s, c, j] if way == PAIR else recv_sem.at[s, c, j], device_id=to, device_id_type=MESH)

    light = core == jnp.where(2 * z < lines, 0, 1)

    def mine_of(z0):
        return jnp.where(z0 == z, light, (core == 0) == (z0 < z))

    def cut(s, c, j):
        return jnp.logical_and(jnp.logical_not(even(s)), (c + 1) * rows <= j * WIDE + narrow)

    def by_width(s, c, j, fn):
        short = cut(s, c, j)
        if_(short, lambda: fn(narrow))
        if_(jnp.logical_not(short), lambda: fn(WIDE))

    def moves(act, s, c, j, up, down, across, pair, arrive):
        def fn(wide):
            if arrive:
                hop(ACROSS, s, c, j, wide).wait_recv()
            for way, cond in ((UP, up), (DOWN, down), (ACROSS, across), (PAIR, pair)):
                if cond is True:
                    act(hop(way, s, c, j, wide))
                elif cond is not False:
                    if_(cond, lambda way=way: act(hop(way, s, c, j, wide)))
        by_width(s, c, j, fn)

    can_up, can_down = z < lines - 1, z > 0
    up, down = jnp.logical_and(can_up, core == 0), jnp.logical_and(can_down, core == 1)

    def own_sends(s, act):
        def one(k):
            j = nth(s, col, k)
            across = jnp.logical_and(k >= turns(s, col), light)
            moves(act, s, col, j, up, down, across, False, False)
        each(blocks(s, col), one)

    def turning(act):
        def of(s):
            if_(light, lambda: each(turns(s, col), lambda k: moves(act, s, col, nth(s, col, k), False, False, True, False, False)))
        return of

    def turn(s, act, arrive):
        c = 2 * z + 1 - y

        if_(light, lambda: each(turns(s, c), lambda k: moves(act, s, c, nth(s, c, k), can_up, can_down, False, True, arrive)))

    def relay(s, d, act, arrive):
        z0 = jnp.where(core == 0, z - d, z + d)

        @pl.when(jnp.logical_and(z0 >= 0, z0 < lines))
        def _():
            near, across_from = 2 * z0 + y, 2 * z0 + 1 - y
            count = blocks(s, near)

            def one(i):
                is_far = i >= count
                c = jnp.where(is_far, across_from, near)
                j = nth(s, c, jnp.where(is_far, i - count, i))
                across = jnp.logical_and(jnp.logical_not(is_far), j < count - turns(s, near))
                moves(act, s, c, j, up, down, across, True, arrive)
            each(count + turns(s, across_from), one)

    def far(s, z0, act, arrive):
        c = 2 * z0 + 1 - y

        def one(j):
            if_(mine_of(z0), lambda: moves(act, s, c, j, False, False, False, True, arrive))
        each(blocks(s, c) - turns(s, c), one)

    def whole(s, z0):
        def wait(c):
            def one(j):
                if_(jnp.logical_not(mine_of(z0)), lambda: by_width(s, c, j, lambda wide: hop(PAIR, s, c, j, wide).wait_recv()))
            each(blocks(s, c), one)
        if_(z0 != z, lambda: wait(2 * z0 + y))
        wait(2 * z0 + 1 - y)

    def span_of(c):
        return pl.ds(c * rows if isinstance(c, int) else pl.multiple_of(c * rows, rows), rows)

    def handed(c):
        return pltpu.make_async_remote_copy(
            src_ref=prior.at[2, span_of(c), :], dst_ref=prior.at[0, span_of(c), :],
            send_sem=prior_send.at[c], recv_sem=prior_recv.at[c],
            device_id={"tm": section + 2}, device_id_type=MESH)

    def stored(l, c):
        return pltpu.make_async_copy(
            prior.at[l + 1, span_of(c), :], out_ref.at[0, span_of(c), half_of(core)], store_sem.at[c])

    def passed(l, c, owner):
        return pltpu.make_async_remote_copy(
            src_ref=prior.at[l + 1, span_of(c), :], dst_ref=out_ref.at[0, span_of(c), half_of(owner)],
            send_sem=out_send.at[c], recv_sem=out_recv.at[c], device_id=sibling, device_id_type=MESH)

    def couple(l, z0):
        span = pl.ds(pl.multiple_of(z0 * plane, plane), plane)
        coupled = jnp.dot(factors[2 * l, span, :], prior[l], preferred_element_type=jnp.float32)
        update[span, :] = (rhs[l, span, :].astype(jnp.float32) - coupled).astype(jnp.bfloat16)

    def solve(l, z0):
        for i in range(lines):
            @pl.when(z0 == i)
            def _(i=i):
                both, lower = slice(i * plane, (i + 1) * plane), slice(i * plane + rows, (i + 1) * plane)
                known, rest = (-(-(2 * i + k) * rows // narrow) * narrow for k in (1, 2))
                result = jnp.dot(factors[2 * l + 1, both, :known], update[:known, :], preferred_element_type=jnp.float32)
                if rest > known:
                    more = jnp.dot(factors[2 * l + 1, lower, known:rest], update[known:rest, :], preferred_element_type=jnp.float32)
                    prior[l + 1, slice(i * plane, i * plane + rows), :] = result[:rows].astype(jnp.bfloat16)
                    prior[l + 1, lower, :] = (result[rows:] + more).astype(jnp.bfloat16)
                else:
                    prior[l + 1, both, :] = result.astype(jnp.bfloat16)
                for c in (2 * i, 2 * i + 1):
                    if_(jnp.logical_and(l == 1, stage < stages - 1), lambda c=c: handed(c).start())
                for c in (2 * i, 2 * i + 1):
                    if_(core == l, lambda c=c: stored(l, c).start())
                    if_(core != l, lambda c=c: passed(l, c, core).start())

    start = lambda copy: copy.start()

    def ready(s):
        l, arr = s // 2, lax.rem(s, 2)
        for a in range(2):
            if_(jnp.logical_and(core == l, arr == a), lambda a=a: own(a).wait())
            if_(jnp.logical_and(core != l, arr == a), lambda a=a: given(a, 1 - core).wait_recv())

    def fetch(s, z0):
        far(s, z0, start, True)

    def work(s, z0):
        @pl.when(first)
        def _():
            whole(s, z0)
            if_(even(s), lambda: couple(s // 2, z0))

            @pl.when(jnp.logical_not(even(s)))
            def _():
                solve(s // 2, z0)

    ready(0)
    turning(start)(0)
    own_sends(0, start)
    given(1, core).start()
    if_(first, own_carry.start)
    own_rhs.start()
    given_rhs(core).start()
    ready(2)
    turning(start)(2)
    ready(1)
    ready(3)
    turning(start)(3)
    own_rhs.wait()
    given_rhs(1 - core).wait_recv()
    if_(first, own_carry.wait)

    steps = 4 * lines

    def in_order(d, fn):
        def side(k, carry):
            z0 = jnp.where(k == 0, z - d, z + d)
            if_(jnp.logical_and(jnp.logical_and(z0 >= 0, z0 < lines), jnp.logical_or(d > 0, k == 0)), lambda: fn(z0))
            return carry
        lax.fori_loop(0, 2, side, 0)

    inside = jnp.logical_and(z > 0, z < lines - 1)
    lag = jnp.where(first, jnp.where(inside, LAGM, LAG), LATE)
    ending = jnp.where(jnp.logical_and(first, jnp.logical_not(inside)), steps - lines + LAST, steps + 99)

    def due(t):
        late = jnp.where(t >= ending, END_LAG, lag)
        return jnp.clip(2 * (t - late), 0, 2 * steps + BEHIND)

    def half_step(h, fn):
        w, k = h // 2, lax.rem(h, 2)
        s, d = w // lines, lax.rem(w, lines)
        z0 = jnp.where(k == 0, z - d, z + d)
        real = jnp.logical_and(jnp.logical_and(h >= 0, h < 2 * steps), jnp.logical_or(d > 0, k == 0))
        if_(jnp.logical_and(real, jnp.logical_and(z0 >= 0, z0 < lines)), lambda: fn(s, z0))

    def step(t, carry):
        s, d = t // lines, lax.rem(t, lines)

        @pl.when(t < steps)
        def _():
            if_(d == 0, lambda: turn(s, start, True))
            if_(d > 0, lambda: relay(s, d, start, True))
            if_(jnp.logical_and(d == lines - AHEAD, s < 3), lambda: own_sends(s + 1, start))

        def item(h, carry):
            half_step(h, fetch)
            half_step(h - BEHIND, work)
            return carry
        lax.fori_loop(due(t), due(t + 1), item, 0)
        return carry
    lax.fori_loop(0, steps + max(LAG, LAGM, LATE) + BEHIND, step, 0)

    sent = lambda copy: copy.wait_send()


    def sends(s):
        turning(sent)(s)
        own_sends(s, sent)
        turn(s, sent, False)
        lax.fori_loop(1, lines, lambda d, carry: (relay(s, d, sent, False), carry)[1], 0)
        each(lines, lambda z0: far(s, z0, sent, False))
    if_(first, lambda: each(4, sends))

    @pl.when(stage > 0)
    def _():
        each(4, lambda s: each(lines, lambda z0: whole(s, z0)))
        staged[...] = rhs[0].astype(jnp.float32)

        def add(k):
            for c in range(2):
                handed(2 * k + c).wait_recv()
            group = pl.ds(pl.multiple_of(k * plane, plane), plane)
            for i in range(pieces):
                span = pl.ds(i * WIDE, WIDE)
                staged[span, :] -= jnp.dot(factors[0, span, group], prior[0, group, :], preferred_element_type=jnp.float32)
        for d in range(max(lines, 4)):
            if d < 4:
                sends(d)
            if d < lines:
                in_order(d, add)
        update[...] = staged[...].astype(jnp.bfloat16)
        each(lines, lambda z0: solve(0, z0))
        for i in range(order // TALL):
            span = slice(i * TALL, (i + 1) * TALL)
            coupled = jnp.dot(factors[2, span, :], prior[1], preferred_element_type=jnp.float32)
            update[span, :] = (rhs[1, span, :].astype(jnp.float32) - coupled).astype(jnp.bfloat16)
        each(lines, lambda z0: solve(1, z0))

    for arr in range(2):
        given(arr, core).wait_send()
    given_rhs(core).wait_send()

    def finish(c):
        for l in range(2):
            if_(core == l, lambda l=l: stored(l, c).wait())
            if_(core != l, lambda l=l: passed(l, c, core).wait_send())
        passed(0, c, 1 - core).wait_recv()
        if_(stage < stages - 1, lambda: handed(c).wait_send())
    each(2 * lines, finish)


def widen(in_ref, out_ref, narrow, wide, load_sem, store_sem):
    rows = narrow.shape[0] // STEPS

    spans = [pl.ds(i * rows, rows) for i in range(STEPS)]
    loads = [pltpu.make_async_copy(in_ref.at[0, s, :], narrow.at[s, :], load_sem.at[i]) for i, s in enumerate(spans)]
    stores = [pltpu.make_async_copy(wide.at[s, :], out_ref.at[0, s, :], store_sem.at[i]) for i, s in enumerate(spans)]
    for load in loads:
        load.start()
    for span, load, store in zip(spans, loads, stores):
        load.wait()
        wide[span, :] = narrow[span, :].astype(jnp.float32)
        store.start()
    for store in stores:
        store.wait()


def shards(stages, cols, inv_diag, sub_diag, rhs, carry_in):
    order, samples = carry_in.shape
    half, lines, pieces = samples // 2, cols // 2, order // WIDE
    flops = 4 * order * order * samples
    result = pl.pallas_call(
        functools.partial(kernel, stages, lines),
        out_shape=jax.ShapeDtypeStruct(rhs.shape, jnp.bfloat16),
        in_specs=[pl.BlockSpec(memory_space=pl.ANY)] * 4,
        out_specs=pl.BlockSpec(memory_space=pl.ANY),
        scratch_shapes=[
            pltpu.VMEM((4, order, order), jnp.bfloat16),
            pltpu.VMEM((2, order, half), jnp.bfloat16),
            pltpu.VMEM((3, order, half), jnp.bfloat16),
            pltpu.VMEM((order, half), jnp.bfloat16),
            pltpu.VMEM((order, half), jnp.float32),
            pltpu.SemaphoreType.DMA((2,)),
            pltpu.SemaphoreType.DMA((3,)),
            pltpu.SemaphoreType.DMA((3,)),
            pltpu.SemaphoreType.DMA,
            pltpu.SemaphoreType.DMA,
            pltpu.SemaphoreType.DMA((4, 4, cols, pieces)),
            pltpu.SemaphoreType.DMA((4, cols, pieces)),
            pltpu.SemaphoreType.DMA((4, cols, pieces)),
            pltpu.SemaphoreType.DMA((cols,)),
            pltpu.SemaphoreType.DMA((cols,)),
            pltpu.SemaphoreType.DMA((cols,)),
            pltpu.SemaphoreType.DMA((cols,)),
            pltpu.SemaphoreType.DMA((cols,)),
        ],
        compiler_params=pltpu.CompilerParams(
            collective_id=0, has_side_effects=True, vmem_limit_bytes=60 * 1024 * 1024),
        cost_estimate=pl.CostEstimate(flops=flops, bytes_accessed=10 * order * samples, transcendentals=0),
    )(inv_diag, sub_diag, rhs, carry_in)
    return pl.pallas_call(
        widen, in_specs=[pl.BlockSpec(memory_space=pl.ANY)], out_specs=pl.BlockSpec(memory_space=pl.ANY),
        scratch_shapes=[
            pltpu.VMEM((order, samples), jnp.bfloat16),
            pltpu.VMEM((order, samples), jnp.float32),
            pltpu.SemaphoreType.DMA((STEPS,)),
            pltpu.SemaphoreType.DMA((STEPS,)),
        ],
        compiler_params=pltpu.CompilerParams(vmem_limit_bytes=WIDEN_MIB * 1024 * 1024),
        out_shape=jax.ShapeDtypeStruct(rhs.shape, jnp.float32),
        cost_estimate=pl.CostEstimate(flops=0, bytes_accessed=6 * order * samples, transcendentals=0),
    )(result)


def solution(mesh):
    in_specs = (
        P("tm", "cols", None),
        P("tm", "cols", None),
        P("tm", None, "cols"),
        P(None, "cols"),
    )
    out_specs = P("tm", None, "cols")
    body = functools.partial(shards, mesh.shape["tm"] // 2, mesh.shape["cols"])
    return jax.shard_map(body, mesh=mesh, in_specs=in_specs, out_specs=out_specs, check_vma=False)
```

```python
import functools

import jax
import jax.numpy as jnp
from jax import lax
from jax.experimental import pallas as pl
from jax.experimental.pallas import tpu as pltpu
from jax.sharding import PartitionSpec as P

MESH = pl.DeviceIdType.MESH
WIDE = 512
UP, DOWN, ACROSS, PAIR = 0, 1, 2, 3
LAG = 3
LAGM = 3
LATE = 6
AHEAD = 1
LAST = 2
END_LAG = 1
BEHIND = 1
TALL = 1024
STEPS = 8
TURNS = [[[3, 0, 0, 0], [4, 0, 0, 0]], [[0, 0, 0, 0], [0, 0, 1, 0]], [[2, 0, 0, 2], [2, 0, 0, 4]], [[1, 0, 0, 0], [1, 0, 0, 0]]]
WIDEN_MIB = 60


def kernel(stages, lines, inv_ref, sub_ref, rhs_ref, carry_ref, out_ref,
           factors, rhs, prior, update, staged,
           own_sem, give_send, give_recv, rhs_sem, carry_sem,
           send_sem, recv_sem, pair_sem, store_sem, out_send, out_recv, prior_send, prior_recv):
    section = lax.axis_index("tm")
    col = lax.axis_index("cols")
    stage, core = section // 2, lax.rem(section, 2)
    z, y = col // 2, lax.rem(col, 2)
    rows, order = inv_ref.shape[1], inv_ref.shape[2]
    half = rhs_ref.shape[2] // 2
    plane, pieces = 2 * rows, order // WIDE
    narrow = WIDE // 2
    sibling = {"tm": 2 * stage + 1 - core}

    def if_(cond, fn):
        pl.when(cond)(fn)

    def each(count, fn):
        def body(j, carry):
            fn(j)
            return carry
        lax.fori_loop(0, count, body, 0)

    mine = pl.ds(pl.multiple_of(col * rows, rows), rows)

    def own(arr):
        return pltpu.make_async_copy((sub_ref, inv_ref)[arr].at[0], factors.at[2 * core + arr, mine, :], own_sem.at[arr])

    def given(arr, owner):
        return pltpu.make_async_remote_copy(
            src_ref=(sub_ref, inv_ref)[arr].at[0], dst_ref=factors.at[2 * owner + arr, mine, :],
            send_sem=give_send.at[arr], recv_sem=give_recv.at[arr], device_id=sibling, device_id_type=MESH)

    def half_of(c):
        return pl.ds(pl.multiple_of(c * half, half), half)

    own_rhs = pltpu.make_async_copy(rhs_ref.at[0, :, half_of(core)], rhs.at[core], rhs_sem)

    def given_rhs(owner):
        return pltpu.make_async_remote_copy(
            src_ref=rhs_ref.at[0, :, half_of(1 - core)], dst_ref=rhs.at[owner],
            send_sem=give_send.at[2], recv_sem=give_recv.at[2], device_id=sibling, device_id_type=MESH)

    own_carry = pltpu.make_async_copy(carry_ref.at[:, half_of(core)], prior.at[0], carry_sem)

    own(0).start()
    own(1).start()

    barrier = pltpu.get_barrier_semaphore()

    def greet(cond, device):
        @pl.when(cond)
        def _():
            pl.semaphore_signal(barrier, inc=1, device_id=device, device_id_type=MESH)

    greet(z > 0, {"cols": col - 2})
    greet(z < lines - 1, {"cols": col + 2})
    pl.semaphore_signal(barrier, inc=1, device_id={"cols": 2 * z + 1 - y}, device_id_type=MESH)
    pl.semaphore_signal(barrier, inc=1, device_id=sibling, device_id_type=MESH)
    greet(stage > 0, {"tm": section - 2})
    greet(stage < stages - 1, {"tm": section + 2})
    ends = [z > 0, z < lines - 1, stage > 0, stage < stages - 1]
    pl.semaphore_wait(barrier, 2 + sum(jnp.where(end, 1, 0) for end in ends))

    given(0, core).start()

    first = stage == 0

    def even(s):
        return lax.rem(s, 2) == 0

    def blocks(s, c):
        return jnp.where(even(s), pieces, (c * rows) // WIDE + 1)

    def turns(s, c):
        z0, y0 = c // 2, lax.rem(c, 2)
        place = jnp.where(z0 == 0, 0, jnp.where(z0 == lines - 1, 3, jnp.where(z0 == 1, 1, 2))) + 4 * y0
        packed = [sum(n << (3 * i) for i, n in enumerate(of[0] + of[1])) for of in TURNS]
        of_stream = jnp.where(s == 0, packed[0], jnp.where(s == 1, packed[1], jnp.where(s == 2, packed[2], packed[3])))
        return jnp.minimum(jnp.right_shift(of_stream, 3 * place) & 7, blocks(s, c))

    def nth(s, c, k):
        return lax.rem(k + blocks(s, c) - turns(s, c), blocks(s, c))

    def hop(way, s, c, j, wide):
        ref = factors.at[s, pl.ds(pl.multiple_of(c * rows, rows), rows), pl.ds(pl.multiple_of(j * WIDE, WIDE), wide)]
        to = ({"tm": 2 * stage, "cols": col + 2}, {"tm": 2 * stage + 1, "cols": col - 2}, {"cols": 2 * z + 1 - y}, sibling)[way]
        return pltpu.make_async_remote_copy(
            src_ref=ref, dst_ref=ref, send_sem=send_sem.at[way, s, c, j],
            recv_sem=pair_sem.at[s, c, j] if way == PAIR else recv_sem.at[s, c, j], device_id=to, device_id_type=MESH)

    light = core == jnp.where(2 * z < lines, 0, 1)

    def mine_of(z0):
        return jnp.where(z0 == z, light, (core == 0) == (z0 < z))

    def cut(s, c, j):
        return jnp.logical_and(jnp.logical_not(even(s)), (c + 1) * rows <= j * WIDE + narrow)

    def by_width(s, c, j, fn):
        short = cut(s, c, j)
        if_(short, lambda: fn(narrow))
        if_(jnp.logical_not(short), lambda: fn(WIDE))

    def moves(act, s, c, j, up, down, across, pair, arrive):
        def fn(wide):
            if arrive:
                hop(ACROSS, s, c, j, wide).wait_recv()
            for way, cond in ((UP, up), (DOWN, down), (ACROSS, across), (PAIR, pair)):
                if cond is True:
                    act(hop(way, s, c, j, wide))
                elif cond is not False:
                    if_(cond, lambda way=way: act(hop(way, s, c, j, wide)))
        by_width(s, c, j, fn)

    can_up, can_down = z < lines - 1, z > 0
    up, down = jnp.logical_and(can_up, core == 0), jnp.logical_and(can_down, core == 1)

    def own_sends(s, act):
        def one(k):
            j = nth(s, col, k)
            across = jnp.logical_and(k >= turns(s, col), light)
            moves(act, s, col, j, up, down, across, False, False)
        each(blocks(s, col), one)

    def turning(act):
        def of(s):
            if_(light, lambda: each(turns(s, col), lambda k: moves(act, s, col, nth(s, col, k), False, False, True, False, False)))
        return of

    def turn(s, act, arrive):
        c = 2 * z + 1 - y

        if_(light, lambda: each(turns(s, c), lambda k: moves(act, s, c, nth(s, c, k), can_up, can_down, False, True, arrive)))

    def relay(s, d, act, arrive):
        z0 = jnp.where(core == 0, z - d, z + d)

        @pl.when(jnp.logical_and(z0 >= 0, z0 < lines))
        def _():
            near, across_from = 2 * z0 + y, 2 * z0 + 1 - y
            count = blocks(s, near)

            def one(i):
                is_far = i >= count
                c = jnp.where(is_far, across_from, near)
                j = nth(s, c, jnp.where(is_far, i - count, i))
                across = jnp.logical_and(jnp.logical_not(is_far), j < count - turns(s, near))
                moves(act, s, c, j, up, down, across, True, arrive)
            each(count + turns(s, across_from), one)

    def far(s, z0, act, arrive):
        c = 2 * z0 + 1 - y

        def one(j):
            if_(mine_of(z0), lambda: moves(act, s, c, j, False, False, False, True, arrive))
        each(blocks(s, c) - turns(s, c), one)

    def whole(s, z0):
        def wait(c):
            def one(j):
                if_(jnp.logical_not(mine_of(z0)), lambda: by_width(s, c, j, lambda wide: hop(PAIR, s, c, j, wide).wait_recv()))
            each(blocks(s, c), one)
        if_(z0 != z, lambda: wait(2 * z0 + y))
        wait(2 * z0 + 1 - y)

    def span_of(c):
        return pl.ds(c * rows if isinstance(c, int) else pl.multiple_of(c * rows, rows), rows)

    def handed(c):
        return pltpu.make_async_remote_copy(
            src_ref=prior.at[2, span_of(c), :], dst_ref=prior.at[0, span_of(c), :],
            send_sem=prior_send.at[c], recv_sem=prior_recv.at[c],
            device_id={"tm": section + 2}, device_id_type=MESH)

    def stored(l, c):
        return pltpu.make_async_copy(
            prior.at[l + 1, span_of(c), :], out_ref.at[0, span_of(c), half_of(core)], store_sem.at[c])

    def passed(l, c, owner):
        return pltpu.make_async_remote_copy(
            src_ref=prior.at[l + 1, span_of(c), :], dst_ref=out_ref.at[0, span_of(c), half_of(owner)],
            send_sem=out_send.at[c], recv_sem=out_recv.at[c], device_id=sibling, device_id_type=MESH)

    def couple(l, z0):
        span = pl.ds(pl.multiple_of(z0 * plane, plane), plane)
        coupled = jnp.dot(factors[2 * l, span, :], prior[l], preferred_element_type=jnp.float32)
        update[span, :] = (rhs[l, span, :].astype(jnp.float32) - coupled).astype(jnp.bfloat16)

    def solve(l, z0):
        for i in range(lines):
            @pl.when(z0 == i)
            def _(i=i):
                both, lower = slice(i * plane, (i + 1) * plane), slice(i * plane + rows, (i + 1) * plane)
                known, rest = (-(-(2 * i + k) * rows // narrow) * narrow for k in (1, 2))
                result = jnp.dot(factors[2 * l + 1, both, :known], update[:known, :], preferred_element_type=jnp.float32)
                if rest > known:
                    more = jnp.dot(factors[2 * l + 1, lower, known:rest], update[known:rest, :], preferred_element_type=jnp.float32)
                    prior[l + 1, slice(i * plane, i * plane + rows), :] = result[:rows].astype(jnp.bfloat16)
                    prior[l + 1, lower, :] = (result[rows:] + more).astype(jnp.bfloat16)
                else:
                    prior[l + 1, both, :] = result.astype(jnp.bfloat16)
                for c in (2 * i, 2 * i + 1):
                    if_(jnp.logical_and(l == 1, stage < stages - 1), lambda c=c: handed(c).start())
                for c in (2 * i, 2 * i + 1):
                    if_(core == l, lambda c=c: stored(l, c).start())
                    if_(core != l, lambda c=c: passed(l, c, core).start())

    start = lambda copy: copy.start()

    def ready(s):
        l, arr = s // 2, lax.rem(s, 2)
        for a in range(2):
            if_(jnp.logical_and(core == l, arr == a), lambda a=a: own(a).wait())
            if_(jnp.logical_and(core != l, arr == a), lambda a=a: given(a, 1 - core).wait_recv())

    def fetch(s, z0):
        far(s, z0, start, True)

    def work(s, z0):
        @pl.when(first)
        def _():
            whole(s, z0)
            if_(even(s), lambda: couple(s // 2, z0))

            @pl.when(jnp.logical_not(even(s)))
            def _():
                solve(s // 2, z0)

    ready(0)
    turning(start)(0)
    own_sends(0, start)
    given(1, core).start()
    if_(first, own_carry.start)
    own_rhs.start()
    given_rhs(core).start()
    ready(2)
    turning(start)(2)
    ready(1)
    turning(start)(1)
    ready(3)
    turning(start)(3)
    own_rhs.wait()
    given_rhs(1 - core).wait_recv()
    if_(first, own_carry.wait)

    steps = 4 * lines

    def in_order(d, fn):
        def side(k, carry):
            z0 = jnp.where(k == 0, z - d, z + d)
            if_(jnp.logical_and(jnp.logical_and(z0 >= 0, z0 < lines), jnp.logical_or(d > 0, k == 0)), lambda: fn(z0))
            return carry
        lax.fori_loop(0, 2, side, 0)

    inside = jnp.logical_and(z > 0, z < lines - 1)
    lag = jnp.where(first, jnp.where(inside, LAGM, LAG), LATE)
    ending = jnp.where(jnp.logical_and(first, jnp.logical_not(inside)), steps - lines + LAST, steps + 99)

    def due(t):
        late = jnp.where(t >= ending, END_LAG, lag)
        return jnp.clip(2 * (t - late), 0, 2 * steps + BEHIND)

    def half_step(h, fn):
        w, k = h // 2, lax.rem(h, 2)
        s, d = w // lines, lax.rem(w, lines)
        z0 = jnp.where(k == 0, z - d, z + d)
        real = jnp.logical_and(jnp.logical_and(h >= 0, h < 2 * steps), jnp.logical_or(d > 0, k == 0))
        if_(jnp.logical_and(real, jnp.logical_and(z0 >= 0, z0 < lines)), lambda: fn(s, z0))

    def step(t, carry):
        s, d = t // lines, lax.rem(t, lines)

        @pl.when(t < steps)
        def _():
            if_(d == 0, lambda: turn(s, start, True))
            if_(d > 0, lambda: relay(s, d, start, True))
            if_(jnp.logical_and(d == lines - AHEAD, s < 3), lambda: own_sends(s + 1, start))

        def item(h, carry):
            half_step(h, fetch)
            half_step(h - BEHIND, work)
            return carry
        lax.fori_loop(due(t), due(t + 1), item, 0)
        return carry
    lax.fori_loop(0, steps + max(LAG, LAGM, LATE) + BEHIND, step, 0)

    sent = lambda copy: copy.wait_send()


    def sends(s):
        turning(sent)(s)
        own_sends(s, sent)
        turn(s, sent, False)
        lax.fori_loop(1, lines, lambda d, carry: (relay(s, d, sent, False), carry)[1], 0)
        each(lines, lambda z0: far(s, z0, sent, False))
    if_(first, lambda: each(4, sends))

    @pl.when(stage > 0)
    def _():
        each(4, lambda s: each(lines, lambda z0: whole(s, z0)))
        staged[...] = rhs[0].astype(jnp.float32)

        def add(k):
            for c in range(2):
                handed(2 * k + c).wait_recv()
            group = pl.ds(pl.multiple_of(k * plane, plane), plane)
            for i in range(pieces):
                span = pl.ds(i * WIDE, WIDE)
                staged[span, :] -= jnp.dot(factors[0, span, group], prior[0, group, :], preferred_element_type=jnp.float32)
        for d in range(max(lines, 4)):
            if d < 4:
                sends(d)
            if d < lines:
                in_order(d, add)
        update[...] = staged[...].astype(jnp.bfloat16)
        each(lines, lambda z0: solve(0, z0))
        for i in range(order // TALL):
            span = slice(i * TALL, (i + 1) * TALL)
            coupled = jnp.dot(factors[2, span, :], prior[1], preferred_element_type=jnp.float32)
            update[span, :] = (rhs[1, span, :].astype(jnp.float32) - coupled).astype(jnp.bfloat16)
        each(lines, lambda z0: solve(1, z0))

    for arr in range(2):
        given(arr, core).wait_send()
    given_rhs(core).wait_send()

    def finish(c):
        for l in range(2):
            if_(core == l, lambda l=l: stored(l, c).wait())
            if_(core != l, lambda l=l: passed(l, c, core).wait_send())
        passed(0, c, 1 - core).wait_recv()
        if_(stage < stages - 1, lambda: handed(c).wait_send())
    each(2 * lines, finish)


def widen(in_ref, out_ref, narrow, wide, load_sem, store_sem):
    rows = narrow.shape[0] // STEPS

    spans = [pl.ds(i * rows, rows) for i in range(STEPS)]
    loads = [pltpu.make_async_copy(in_ref.at[0, s, :], narrow.at[s, :], load_sem.at[i]) for i, s in enumerate(spans)]
    stores = [pltpu.make_async_copy(wide.at[s, :], out_ref.at[0, s, :], store_sem.at[i]) for i, s in enumerate(spans)]
    for load in loads:
        load.start()
    for span, load, store in zip(spans, loads, stores):
        load.wait()
        wide[span, :] = narrow[span, :].astype(jnp.float32)
        store.start()
    for store in stores:
        store.wait()


def shards(stages, cols, inv_diag, sub_diag, rhs, carry_in):
    order, samples = carry_in.shape
    half, lines, pieces = samples // 2, cols // 2, order // WIDE
    flops = 4 * order * order * samples
    result = pl.pallas_call(
        functools.partial(kernel, stages, lines),
        out_shape=jax.ShapeDtypeStruct(rhs.shape, jnp.bfloat16),
        in_specs=[pl.BlockSpec(memory_space=pl.ANY)] * 4,
        out_specs=pl.BlockSpec(memory_space=pl.ANY),
        scratch_shapes=[
            pltpu.VMEM((4, order, order), jnp.bfloat16),
            pltpu.VMEM((2, order, half), jnp.bfloat16),
            pltpu.VMEM((3, order, half), jnp.bfloat16),
            pltpu.VMEM((order, half), jnp.bfloat16),
            pltpu.VMEM((order, half), jnp.float32),
            pltpu.SemaphoreType.DMA((2,)),
            pltpu.SemaphoreType.DMA((3,)),
            pltpu.SemaphoreType.DMA((3,)),
            pltpu.SemaphoreType.DMA,
            pltpu.SemaphoreType.DMA,
            pltpu.SemaphoreType.DMA((4, 4, cols, pieces)),
            pltpu.SemaphoreType.DMA((4, cols, pieces)),
            pltpu.SemaphoreType.DMA((4, cols, pieces)),
            pltpu.SemaphoreType.DMA((cols,)),
            pltpu.SemaphoreType.DMA((cols,)),
            pltpu.SemaphoreType.DMA((cols,)),
            pltpu.SemaphoreType.DMA((cols,)),
            pltpu.SemaphoreType.DMA((cols,)),
        ],
        compiler_params=pltpu.CompilerParams(
            collective_id=0, has_side_effects=True, vmem_limit_bytes=60 * 1024 * 1024),
        cost_estimate=pl.CostEstimate(flops=flops, bytes_accessed=10 * order * samples, transcendentals=0),
    )(inv_diag, sub_diag, rhs, carry_in)
    return pl.pallas_call(
        widen, in_specs=[pl.BlockSpec(memory_space=pl.ANY)], out_specs=pl.BlockSpec(memory_space=pl.ANY),
        scratch_shapes=[
            pltpu.VMEM((order, samples), jnp.bfloat16),
            pltpu.VMEM((order, samples), jnp.float32),
            pltpu.SemaphoreType.DMA((STEPS,)),
            pltpu.SemaphoreType.DMA((STEPS,)),
        ],
        compiler_params=pltpu.CompilerParams(vmem_limit_bytes=WIDEN_MIB * 1024 * 1024),
        out_shape=jax.ShapeDtypeStruct(rhs.shape, jnp.float32),
        cost_estimate=pl.CostEstimate(flops=0, bytes_accessed=6 * order * samples, transcendentals=0),
    )(result)


def solution(mesh):
    in_specs = (
        P("tm", "cols", None),
        P("tm", "cols", None),
        P("tm", None, "cols"),
        P(None, "cols"),
    )
    out_specs = P("tm", None, "cols")
    body = functools.partial(shards, mesh.shape["tm"] // 2, mesh.shape["cols"])
    return jax.shard_map(body, mesh=mesh, in_specs=in_specs, out_specs=out_specs, check_vma=False)
```

```python
import functools

import jax
import jax.numpy as jnp
from jax import lax
from jax.experimental import pallas as pl
from jax.experimental.pallas import tpu as pltpu
from jax.sharding import PartitionSpec as P

MESH = pl.DeviceIdType.MESH
WIDE = 512
UP, DOWN, ACROSS, PAIR = 0, 1, 2, 3
LAG = 3
LAGM = 3
LATE = 6
AHEAD = 1
LAST = 2
END_LAG = 1
BEHIND = 1
TALL = 1024
STEPS = 8
TURNS = [[[3, 0, 0, 0], [4, 0, 0, 0]], [[0, 0, 0, 0], [0, 0, 0, 0]], [[2, 0, 0, 2], [3, 0, 0, 3]], [[1, 0, 0, 0], [1, 0, 0, 0]]]
WIDEN_MIB = 60


def kernel(stages, lines, inv_ref, sub_ref, rhs_ref, carry_ref, out_ref,
           factors, rhs, prior, update, staged,
           own_sem, give_send, give_recv, rhs_sem, carry_sem,
           send_sem, recv_sem, pair_sem, store_sem, out_send, out_recv, prior_send, prior_recv):
    section = lax.axis_index("tm")
    col = lax.axis_index("cols")
    stage, core = section // 2, lax.rem(section, 2)
    z, y = col // 2, lax.rem(col, 2)
    rows, order = inv_ref.shape[1], inv_ref.shape[2]
    half = rhs_ref.shape[2] // 2
    plane, pieces = 2 * rows, order // WIDE
    narrow = WIDE // 2
    sibling = {"tm": 2 * stage + 1 - core}

    def if_(cond, fn):
        pl.when(cond)(fn)

    def each(count, fn):
        def body(j, carry):
            fn(j)
            return carry
        lax.fori_loop(0, count, body, 0)

    mine = pl.ds(pl.multiple_of(col * rows, rows), rows)

    def own(arr):
        return pltpu.make_async_copy((sub_ref, inv_ref)[arr].at[0], factors.at[2 * core + arr, mine, :], own_sem.at[arr])

    def given(arr, owner):
        return pltpu.make_async_remote_copy(
            src_ref=(sub_ref, inv_ref)[arr].at[0], dst_ref=factors.at[2 * owner + arr, mine, :],
            send_sem=give_send.at[arr], recv_sem=give_recv.at[arr], device_id=sibling, device_id_type=MESH)

    def half_of(c):
        return pl.ds(pl.multiple_of(c * half, half), half)

    own_rhs = pltpu.make_async_copy(rhs_ref.at[0, :, half_of(core)], rhs.at[core], rhs_sem)

    def given_rhs(owner):
        return pltpu.make_async_remote_copy(
            src_ref=rhs_ref.at[0, :, half_of(1 - core)], dst_ref=rhs.at[owner],
            send_sem=give_send.at[2], recv_sem=give_recv.at[2], device_id=sibling, device_id_type=MESH)

    own_carry = pltpu.make_async_copy(carry_ref.at[:, half_of(core)], prior.at[0], carry_sem)

    own(0).start()
    own(1).start()

    barrier = pltpu.get_barrier_semaphore()

    def greet(cond, device):
        @pl.when(cond)
        def _():
            pl.semaphore_signal(barrier, inc=1, device_id=device, device_id_type=MESH)

    greet(z > 0, {"cols": col - 2})
    greet(z < lines - 1, {"cols": col + 2})
    pl.semaphore_signal(barrier, inc=1, device_id={"cols": 2 * z + 1 - y}, device_id_type=MESH)
    pl.semaphore_signal(barrier, inc=1, device_id=sibling, device_id_type=MESH)
    greet(stage > 0, {"tm": section - 2})
    greet(stage < stages - 1, {"tm": section + 2})
    ends = [z > 0, z < lines - 1, stage > 0, stage < stages - 1]
    pl.semaphore_wait(barrier, 2 + sum(jnp.where(end, 1, 0) for end in ends))

    given(0, core).start()

    first = stage == 0

    def even(s):
        return lax.rem(s, 2) == 0

    def blocks(s, c):
        return jnp.where(even(s), pieces, (c * rows) // WIDE + 1)

    def turns(s, c):
        z0, y0 = c // 2, lax.rem(c, 2)
        place = jnp.where(z0 == 0, 0, jnp.where(z0 == lines - 1, 3, jnp.where(z0 == 1, 1, 2))) + 4 * y0
        packed = [sum(n << (3 * i) for i, n in enumerate(of[0] + of[1])) for of in TURNS]
        of_stream = jnp.where(s == 0, packed[0], jnp.where(s == 1, packed[1], jnp.where(s == 2, packed[2], packed[3])))
        return jnp.minimum(jnp.right_shift(of_stream, 3 * place) & 7, blocks(s, c))

    def nth(s, c, k):
        return lax.rem(k + blocks(s, c) - turns(s, c), blocks(s, c))

    def hop(way, s, c, j, wide):
        ref = factors.at[s, pl.ds(pl.multiple_of(c * rows, rows), rows), pl.ds(pl.multiple_of(j * WIDE, WIDE), wide)]
        to = ({"tm": 2 * stage, "cols": col + 2}, {"tm": 2 * stage + 1, "cols": col - 2}, {"cols": 2 * z + 1 - y}, sibling)[way]
        return pltpu.make_async_remote_copy(
            src_ref=ref, dst_ref=ref, send_sem=send_sem.at[way, s, c, j],
            recv_sem=pair_sem.at[s, c, j] if way == PAIR else recv_sem.at[s, c, j], device_id=to, device_id_type=MESH)

    light = core == jnp.where(2 * z < lines, 0, 1)

    def mine_of(z0):
        return jnp.where(z0 == z, light, (core == 0) == (z0 < z))

    def cut(s, c, j):
        return jnp.logical_and(jnp.logical_not(even(s)), (c + 1) * rows <= j * WIDE + narrow)

    def by_width(s, c, j, fn):
        short = cut(s, c, j)
        if_(short, lambda: fn(narrow))
        if_(jnp.logical_not(short), lambda: fn(WIDE))

    def moves(act, s, c, j, up, down, across, pair, arrive):
        def fn(wide):
            if arrive:
                hop(ACROSS, s, c, j, wide).wait_recv()
            for way, cond in ((UP, up), (DOWN, down), (ACROSS, across), (PAIR, pair)):
                if cond is True:
                    act(hop(way, s, c, j, wide))
                elif cond is not False:
                    if_(cond, lambda way=way: act(hop(way, s, c, j, wide)))
        by_width(s, c, j, fn)

    can_up, can_down = z < lines - 1, z > 0
    up, down = jnp.logical_and(can_up, core == 0), jnp.logical_and(can_down, core == 1)

    def own_sends(s, act):
        def one(k):
            j = nth(s, col, k)
            across = jnp.logical_and(k >= turns(s, col), light)
            moves(act, s, col, j, up, down, across, False, False)
        each(blocks(s, col), one)

    def turning(act):
        def of(s):
            if_(light, lambda: each(turns(s, col), lambda k: moves(act, s, col, nth(s, col, k), False, False, True, False, False)))
        return of

    def turn(s, act, arrive):
        c = 2 * z + 1 - y

        if_(light, lambda: each(turns(s, c), lambda k: moves(act, s, c, nth(s, c, k), can_up, can_down, False, True, arrive)))

    def relay(s, d, act, arrive):
        z0 = jnp.where(core == 0, z - d, z + d)

        @pl.when(jnp.logical_and(z0 >= 0, z0 < lines))
        def _():
            near, across_from = 2 * z0 + y, 2 * z0 + 1 - y
            count = blocks(s, near)

            def one(i):
                is_far = i >= count
                c = jnp.where(is_far, across_from, near)
                j = nth(s, c, jnp.where(is_far, i - count, i))
                across = jnp.logical_and(jnp.logical_not(is_far), j < count - turns(s, near))
                moves(act, s, c, j, up, down, across, True, arrive)
            each(count + turns(s, across_from), one)

    def far(s, z0, act, arrive):
        c = 2 * z0 + 1 - y

        def one(j):
            if_(mine_of(z0), lambda: moves(act, s, c, j, False, False, False, True, arrive))
        each(blocks(s, c) - turns(s, c), one)

    def whole(s, z0):
        def wait(c):
            def one(j):
                if_(jnp.logical_not(mine_of(z0)), lambda: by_width(s, c, j, lambda wide: hop(PAIR, s, c, j, wide).wait_recv()))
            each(blocks(s, c), one)
        if_(z0 != z, lambda: wait(2 * z0 + y))
        wait(2 * z0 + 1 - y)

    def span_of(c):
        return pl.ds(c * rows if isinstance(c, int) else pl.multiple_of(c * rows, rows), rows)

    def handed(c):
        return pltpu.make_async_remote_copy(
            src_ref=prior.at[2, span_of(c), :], dst_ref=prior.at[0, span_of(c), :],
            send_sem=prior_send.at[c], recv_sem=prior_recv.at[c],
            device_id={"tm": section + 2}, device_id_type=MESH)

    def stored(l, c):
        return pltpu.make_async_copy(
            prior.at[l + 1, span_of(c), :], out_ref.at[0, span_of(c), half_of(core)], store_sem.at[c])

    def passed(l, c, owner):
        return pltpu.make_async_remote_copy(
            src_ref=prior.at[l + 1, span_of(c), :], dst_ref=out_ref.at[0, span_of(c), half_of(owner)],
            send_sem=out_send.at[c], recv_sem=out_recv.at[c], device_id=sibling, device_id_type=MESH)

    def couple(l, z0):
        span = pl.ds(pl.multiple_of(z0 * plane, plane), plane)
        coupled = jnp.dot(factors[2 * l, span, :], prior[l], preferred_element_type=jnp.float32)
        update[span, :] = (rhs[l, span, :].astype(jnp.float32) - coupled).astype(jnp.bfloat16)

    def solve(l, z0):
        for i in range(lines):
            @pl.when(z0 == i)
            def _(i=i):
                both, lower = slice(i * plane, (i + 1) * plane), slice(i * plane + rows, (i + 1) * plane)
                known, rest = (-(-(2 * i + k) * rows // narrow) * narrow for k in (1, 2))
                result = jnp.dot(factors[2 * l + 1, both, :known], update[:known, :], preferred_element_type=jnp.float32)
                if rest > known:
                    more = jnp.dot(factors[2 * l + 1, lower, known:rest], update[known:rest, :], preferred_element_type=jnp.float32)
                    prior[l + 1, slice(i * plane, i * plane + rows), :] = result[:rows].astype(jnp.bfloat16)
                    prior[l + 1, lower, :] = (result[rows:] + more).astype(jnp.bfloat16)
                else:
                    prior[l + 1, both, :] = result.astype(jnp.bfloat16)
                for c in (2 * i, 2 * i + 1):
                    if_(jnp.logical_and(l == 1, stage < stages - 1), lambda c=c: handed(c).start())
                for c in (2 * i, 2 * i + 1):
                    if_(core == l, lambda c=c: stored(l, c).start())
                    if_(core != l, lambda c=c: passed(l, c, core).start())

    start = lambda copy: copy.start()

    def ready(s):
        l, arr = s // 2, lax.rem(s, 2)
        for a in range(2):
            if_(jnp.logical_and(core == l, arr == a), lambda a=a: own(a).wait())
            if_(jnp.logical_and(core != l, arr == a), lambda a=a: given(a, 1 - core).wait_recv())

    def fetch(s, z0):
        far(s, z0, start, True)

    def work(s, z0):
        @pl.when(first)
        def _():
            whole(s, z0)
            if_(even(s), lambda: couple(s // 2, z0))

            @pl.when(jnp.logical_not(even(s)))
            def _():
                solve(s // 2, z0)

    ready(0)
    turning(start)(0)
    own_sends(0, start)
    given(1, core).start()
    if_(first, own_carry.start)
    own_rhs.start()
    given_rhs(core).start()
    ready(2)
    turning(start)(2)
    ready(1)
    turning(start)(1)
    ready(3)
    turning(start)(3)
    own_rhs.wait()
    given_rhs(1 - core).wait_recv()
    if_(first, own_carry.wait)

    steps = 4 * lines

    def in_order(d, fn):
        def side(k, carry):
            z0 = jnp.where(k == 0, z - d, z + d)
            if_(jnp.logical_and(jnp.logical_and(z0 >= 0, z0 < lines), jnp.logical_or(d > 0, k == 0)), lambda: fn(z0))
            return carry
        lax.fori_loop(0, 2, side, 0)

    inside = jnp.logical_and(z > 0, z < lines - 1)
    lag = jnp.where(first, jnp.where(inside, LAGM, LAG), LATE)
    ending = jnp.where(jnp.logical_and(first, jnp.logical_not(inside)), steps - lines + LAST, steps + 99)

    def due(t):
        late = jnp.where(t >= ending, END_LAG, lag)
        return jnp.clip(2 * (t - late), 0, 2 * steps + BEHIND)

    def half_step(h, fn):
        w, k = h // 2, lax.rem(h, 2)
        s, d = w // lines, lax.rem(w, lines)
        z0 = jnp.where(k == 0, z - d, z + d)
        real = jnp.logical_and(jnp.logical_and(h >= 0, h < 2 * steps), jnp.logical_or(d > 0, k == 0))
        if_(jnp.logical_and(real, jnp.logical_and(z0 >= 0, z0 < lines)), lambda: fn(s, z0))

    def step(t, carry):
        s, d = t // lines, lax.rem(t, lines)

        @pl.when(t < steps)
        def _():
            if_(d == 0, lambda: turn(s, start, True))
            if_(d > 0, lambda: relay(s, d, start, True))
            if_(jnp.logical_and(d == lines - AHEAD, s < 3), lambda: own_sends(s + 1, start))

        def item(h, carry):
            half_step(h, fetch)
            half_step(h - BEHIND, work)
            return carry
        lax.fori_loop(due(t), due(t + 1), item, 0)
        return carry
    lax.fori_loop(0, steps + max(LAG, LAGM, LATE) + BEHIND, step, 0)

    sent = lambda copy: copy.wait_send()


    def sends(s):
        turning(sent)(s)
        own_sends(s, sent)
        turn(s, sent, False)
        lax.fori_loop(1, lines, lambda d, carry: (relay(s, d, sent, False), carry)[1], 0)
        each(lines, lambda z0: far(s, z0, sent, False))
    if_(first, lambda: each(4, sends))

    @pl.when(stage > 0)
    def _():
        each(4, lambda s: each(lines, lambda z0: whole(s, z0)))
        staged[...] = rhs[0].astype(jnp.float32)

        def add(k):
            for c in range(2):
                handed(2 * k + c).wait_recv()
            group = pl.ds(pl.multiple_of(k * plane, plane), plane)
            for i in range(pieces):
                span = pl.ds(i * WIDE, WIDE)
                staged[span, :] -= jnp.dot(factors[0, span, group], prior[0, group, :], preferred_element_type=jnp.float32)
        for d in range(max(lines, 4)):
            if d < 4:
                sends(d)
            if d < lines:
                in_order(d, add)
        update[...] = staged[...].astype(jnp.bfloat16)
        each(lines, lambda z0: solve(0, z0))
        for i in range(order // TALL):
            span = slice(i * TALL, (i + 1) * TALL)
            coupled = jnp.dot(factors[2, span, :], prior[1], preferred_element_type=jnp.float32)
            update[span, :] = (rhs[1, span, :].astype(jnp.float32) - coupled).astype(jnp.bfloat16)
        each(lines, lambda z0: solve(1, z0))

    for arr in range(2):
        given(arr, core).wait_send()
    given_rhs(core).wait_send()

    def finish(c):
        for l in range(2):
            if_(core == l, lambda l=l: stored(l, c).wait())
            if_(core != l, lambda l=l: passed(l, c, core).wait_send())
        passed(0, c, 1 - core).wait_recv()
        if_(stage < stages - 1, lambda: handed(c).wait_send())
    each(2 * lines, finish)


def widen(in_ref, out_ref, narrow, wide, load_sem, store_sem):
    rows = narrow.shape[0] // STEPS

    spans = [pl.ds(i * rows, rows) for i in range(STEPS)]
    loads = [pltpu.make_async_copy(in_ref.at[0, s, :], narrow.at[s, :], load_sem.at[i]) for i, s in enumerate(spans)]
    stores = [pltpu.make_async_copy(wide.at[s, :], out_ref.at[0, s, :], store_sem.at[i]) for i, s in enumerate(spans)]
    for load in loads:
        load.start()
    for span, load, store in zip(spans, loads, stores):
        load.wait()
        wide[span, :] = narrow[span, :].astype(jnp.float32)
        store.start()
    for store in stores:
        store.wait()


def shards(stages, cols, inv_diag, sub_diag, rhs, carry_in):
    order, samples = carry_in.shape
    half, lines, pieces = samples // 2, cols // 2, order // WIDE
    flops = 4 * order * order * samples
    result = pl.pallas_call(
        functools.partial(kernel, stages, lines),
        out_shape=jax.ShapeDtypeStruct(rhs.shape, jnp.bfloat16),
        in_specs=[pl.BlockSpec(memory_space=pl.ANY)] * 4,
        out_specs=pl.BlockSpec(memory_space=pl.ANY),
        scratch_shapes=[
            pltpu.VMEM((4, order, order), jnp.bfloat16),
            pltpu.VMEM((2, order, half), jnp.bfloat16),
            pltpu.VMEM((3, order, half), jnp.bfloat16),
            pltpu.VMEM((order, half), jnp.bfloat16),
            pltpu.VMEM((order, half), jnp.float32),
            pltpu.SemaphoreType.DMA((2,)),
            pltpu.SemaphoreType.DMA((3,)),
            pltpu.SemaphoreType.DMA((3,)),
            pltpu.SemaphoreType.DMA,
            pltpu.SemaphoreType.DMA,
            pltpu.SemaphoreType.DMA((4, 4, cols, pieces)),
            pltpu.SemaphoreType.DMA((4, cols, pieces)),
            pltpu.SemaphoreType.DMA((4, cols, pieces)),
            pltpu.SemaphoreType.DMA((cols,)),
            pltpu.SemaphoreType.DMA((cols,)),
            pltpu.SemaphoreType.DMA((cols,)),
            pltpu.SemaphoreType.DMA((cols,)),
            pltpu.SemaphoreType.DMA((cols,)),
        ],
        compiler_params=pltpu.CompilerParams(
            collective_id=0, has_side_effects=True, vmem_limit_bytes=60 * 1024 * 1024),
        cost_estimate=pl.CostEstimate(flops=flops, bytes_accessed=10 * order * samples, transcendentals=0),
    )(inv_diag, sub_diag, rhs, carry_in)
    return pl.pallas_call(
        widen, in_specs=[pl.BlockSpec(memory_space=pl.ANY)], out_specs=pl.BlockSpec(memory_space=pl.ANY),
        scratch_shapes=[
            pltpu.VMEM((order, samples), jnp.bfloat16),
            pltpu.VMEM((order, samples), jnp.float32),
            pltpu.SemaphoreType.DMA((STEPS,)),
            pltpu.SemaphoreType.DMA((STEPS,)),
        ],
        compiler_params=pltpu.CompilerParams(vmem_limit_bytes=WIDEN_MIB * 1024 * 1024),
        out_shape=jax.ShapeDtypeStruct(rhs.shape, jnp.float32),
        cost_estimate=pl.CostEstimate(flops=0, bytes_accessed=6 * order * samples, transcendentals=0),
    )(result)


def solution(mesh):
    in_specs = (
        P("tm", "cols", None),
        P("tm", "cols", None),
        P("tm", None, "cols"),
        P(None, "cols"),
    )
    out_specs = P("tm", None, "cols")
    body = functools.partial(shards, mesh.shape["tm"] // 2, mesh.shape["cols"])
    return jax.shard_map(body, mesh=mesh, in_specs=in_specs, out_specs=out_specs, check_vma=False)
```
